256 devices in a mesh: rows: 64 (over z, y, core), tp: 4 (over x).
Axes of the slice: x: 4, y: 4, z: 8, core: 2. Of those that a mesh axis runs over, the one named last changes fastest.
Arguments:
- state_in: float32 [128, 64, 128, 256], P('rows', 'tp'), may hold values from -8 to 8
- tail_x: bfloat16 [128, 3, 64, 128], P('rows', None, 'tp'), may hold values from -6 to 6
- tail_bc: bfloat16 [128, 3, 2, 4, 256], P('rows'), may hold values from -6 to 6
- source: int32 [128], replicated, may hold values from 0 to 127, as said below
- active: int32 [128], P('rows'), may hold values 0 or 1
- x_new: bfloat16 [2, 128, 64, 128], P(None, 'rows', 'tp'), may hold values from -6 to 6
- z_new: bfloat16 [2, 128, 64, 128], P(None, 'rows', 'tp'), may hold values from -6 to 6
- bc_new: bfloat16 [2, 128, 2, 4, 256], P(None, 'rows'), may hold values from -6 to 6
- dt_new: float32 [2, 128, 128], P(None, 'rows'), may hold values from -6 to 6
- conv_wx: float32 [4, 64, 128], P(None, 'tp'), may hold values from -3 to 3
- conv_bx: float32 [64, 128], P('tp'), may hold values from -2 to 2
- conv_wbc: float32 [4, 2, 4, 256], replicated, may hold values from -3 to 3
- conv_bbc: float32 [2, 4, 256], replicated, may hold values from -2 to 2
- dt_bias: float32 [128], replicated, may hold values from -4 to -1
- a_log: float32 [128], replicated, may hold values from 0 to 2.5
- skip_d: float32 [128], replicated, may hold values from 0.5 to 2
- norm_gain: float32 [64, 128], P('tp'), may hold values from 0.1 to 1.9
Outputs:
- state_out: float32 [128, 64, 128, 256], P('rows', 'tp')
- tail_x_out: bfloat16 [128, 3, 64, 128], P('rows', None, 'tp')
- tail_bc_out: bfloat16 [128, 3, 2, 4, 256], P('rows')
- y_out: bfloat16 [2, 128, 64, 128], P(None, 'rows', 'tp')
The draws below stay inside these ranges and needn't reach their ends.
Inputs may be any that keep to these rules, and one draw needn't show every extreme that they name: source is a permutation of the 128 slots; on each index of rows at most 1 of its 2 slots take a row held on another index, and as many give one away.
All inputs are finite; a program needn't handle non-finite values. No bound on the sum of `active` on one device may be relied on, other than what follows from the above.
Results may differ from the reference program's by a relative error of at most 0.0012.
Values sent between devices are 32-bit elements; how exact they have to be, the bound alone decides.
A program may use at most 128 MiB of HBM per device.

```python
import math
import jax
import jax.numpy as jnp
from jax import lax

H = 128
P_SIZE = 64
N = 256
HG = 32
STEPS = 2
MOVE = 1
SLOT_DEV = 2
G = 4
SLOTS = 128


def draw_state_in(key, part):
    key = jax.random.fold_in(key, 5)
    first_key, second_key = jax.random.split(key)
    levels = jax.random.uniform(second_key, (P_SIZE, 1, 1), minval=0.0, maxval=1.0)
    scales = jnp.exp(levels * math.log(10.0)) * (2.0 / math.sqrt(N))
    basis = jnp.clip(jax.random.normal(first_key, (SLOTS, P_SIZE, H, N)), -6.0, 6.0)
    return jnp.clip(basis * scales, -8.0, 8.0).astype(jnp.float32)


def shuffled(subkey):
    return jax.random.permutation(subkey, SLOT_DEV)


def draw_source(key, part):
    key = jax.random.fold_in(key, 11)
    devices = SLOTS // SLOT_DEV
    keys = jax.random.split(key, MOVE + 2)
    order = jax.vmap(shuffled)(jax.random.split(keys[0], devices))
    source = jnp.arange(SLOTS, dtype=jnp.int32)
    for lane_index in range(MOVE):
        cycle = jax.random.permutation(keys[lane_index + 1], devices)
        follow = jnp.roll(cycle, -1)
        giver = cycle * SLOT_DEV + order[cycle, lane_index]
        taker = follow * SLOT_DEV + order[follow, lane_index]
        source = source.at[taker].set(giver)
    mixing = jax.vmap(shuffled)(jax.random.split(keys[MOVE + 1], devices))
    layout = (jnp.arange(devices, dtype=jnp.int32)[:, None] * SLOT_DEV + mixing).reshape(-1)
    return source[layout].astype(jnp.int32)


def plant(array, stream_key, smallest, top_value):
    longest = array.shape.index(max(array.shape))
    spots = []
    for shift in (0, 1):
        where = [jax.random.randint(jax.random.fold_in(stream_key, axis), (), 0, length) for axis, length in enumerate(array.shape)]
        where[longest] = (where[longest] + shift) % array.shape[longest]
        spots.append(tuple(where))
    return array.at[spots[0]].set(smallest).at[spots[1]].set(top_value)


def block_scale(rng, dims, shards, least, high):
    def one(axis_at, shards_of):
        heights = jax.random.uniform(jax.random.fold_in(jax.random.fold_in(rng, 6), axis_at), (shards_of,), jnp.float32, least / len(shards), high / len(shards))
        return jnp.repeat(jnp.exp(heights), dims[axis_at] // shards_of).reshape((-1,) + (1,) * (len(dims) - axis_at - 1))

    gain = one(*shards[0])
    for cut in shards[1:]:
        gain = gain * one(*cut)
    return gain


def scatter_about(rng, dims, deviation, limit, shards=(), kind=jnp.bfloat16):
    entries = jax.random.normal(rng, dims, jnp.float32) * deviation
    if len(shards) > 0:
        entries = block_scale(rng, dims, shards, -0.22, 0.18) * entries
    return jnp.clip(entries, min=-limit, max=limit).astype(kind)


def setup_inputs(seed: int = 0) -> dict:
    key_of = jax.random.split(jax.random.key(seed), 18)
    return {
        "state_in": draw_state_in(jax.random.fold_in(key_of[17], 71), 0),
        "tail_x": scatter_about(key_of[1], (SLOTS, 3, P_SIZE, H), 1.0, 6.0, ((0, 64), (2, 4))),
        "tail_bc": scatter_about(key_of[2], (SLOTS, 3, 2, G, N), 1.0, 6.0, ((0, 64),)),
        "source": draw_source(jax.random.fold_in(key_of[17], 71), 0),
        "active": plant((jax.random.randint(key_of[4], (SLOTS,), 0, 4) < 3).astype(jnp.int32), jax.random.fold_in(key_of[4], 1), 0, 1),
        "x_new": scatter_about(key_of[5], (STEPS, SLOTS, P_SIZE, H), 1.0, 6.0, ((1, 64), (2, 4))),
        "z_new": scatter_about(key_of[6], (STEPS, SLOTS, P_SIZE, H), 1.0, 6.0, ((1, 64), (2, 4))),
        "bc_new": scatter_about(key_of[7], (STEPS, SLOTS, 2, G, N), 1.0, 6.0, ((1, 64),)),
        "dt_new": scatter_about(key_of[8], (STEPS, SLOTS, H), 1.0, 6.0, ((1, 64),), jnp.float32),
        "conv_wx": scatter_about(key_of[9], (4, P_SIZE, H), 0.5, 3.0, ((1, 4),), jnp.float32),
        "conv_bx": scatter_about(key_of[10], (P_SIZE, H), 0.3, 2.0, ((0, 4),), jnp.float32),
        "conv_wbc": scatter_about(key_of[11], (4, 2, G, N), 0.5, 3.0, (), jnp.float32),
        "conv_bbc": scatter_about(key_of[12], (2, G, N), 0.3, 2.0, (), jnp.float32),
        "dt_bias": jnp.clip(jax.random.uniform(key_of[13], (H,), jnp.float32, -4.0, -1.0), -4.0, -1.0),
        "a_log": jnp.clip(jax.random.uniform(key_of[14], (H,), jnp.float32, 0.0, 2.5), 0.0, 2.5),
        "skip_d": jnp.clip(jax.random.uniform(key_of[15], (H,), jnp.float32, 0.5, 2.0), 0.5, 2.0),
        "norm_gain": jnp.clip(1.0 + 0.18 * jax.random.normal(key_of[16], (P_SIZE, H), jnp.float32), 0.1, 1.9),
    }


EPSILON = 1e-05

def reference(state_in, tail_x, tail_bc, source, active, x_new, z_new, bc_new, dt_new, conv_wx, conv_bx, conv_wbc, conv_bbc, dt_bias, a_log, skip_d, norm_gain):
    rate = jnp.exp(a_log)

    def per_slot(items):
        anchor, is_live, slot_x, slot_z, slot_bc, slot_dt = items
        state = lax.dynamic_index_in_dim(state_in, anchor, 0, keepdims=False)
        window_x = lax.dynamic_index_in_dim(tail_x, anchor, 0, keepdims=False)
        window_bc = lax.dynamic_index_in_dim(tail_bc, anchor, 0, keepdims=False)
        live = is_live == 1
        outputs = []
        for step_index in range(STEPS):
            entry_x = slot_x[step_index]
            entry_bc = slot_bc[step_index]
            frame_x = jnp.concatenate([window_x, entry_x[None]], axis=0).astype(jnp.float32)
            conv_x = jax.nn.silu(lax.optimization_barrier(jnp.sum(frame_x * conv_wx, axis=0)) + conv_bx)
            frame_bc = jnp.concatenate([window_bc, entry_bc[None]], axis=0).astype(jnp.float32)
            conv_bc = jax.nn.silu(lax.optimization_barrier(jnp.sum(frame_bc * conv_wbc, axis=0)) + conv_bbc)
            expand_b = jnp.repeat(conv_bc[0], HG, axis=0)
            expand_c = jnp.repeat(conv_bc[1], HG, axis=0)
            step_size = jax.nn.softplus(slot_dt[step_index] + dt_bias)
            decay = jnp.exp(-step_size * rate)
            candidate = state * decay[None, :, None] + (step_size[None, :] * conv_x)[:, :, None] * expand_b[None]
            readout = lax.optimization_barrier(jnp.sum(candidate * expand_c[None], axis=-1)) + skip_d * conv_x
            gated = readout * jax.nn.silu(slot_z[step_index].astype(jnp.float32))
            mean_sq = lax.optimization_barrier(jnp.mean(jnp.square(gated).reshape(P_SIZE, G, HG), axis=(0, 2)))
            factor = lax.rsqrt(mean_sq + EPSILON)
            scaled = gated * jnp.repeat(factor, HG)[None, :] * norm_gain
            outputs.append(jnp.where(live, scaled, 0.0).astype(jnp.bfloat16))
            state = jnp.where(live, candidate, state)
            window_x = jnp.where(live, jnp.concatenate([window_x[1:], entry_x[None]], axis=0), window_x)
            window_bc = jnp.where(live, jnp.concatenate([window_bc[1:], entry_bc[None]], axis=0), window_bc)
        return (state, window_x, window_bc, jnp.stack(outputs))
    slot_inputs = (source, active, jnp.swapaxes(x_new, 0, 1), jnp.swapaxes(z_new, 0, 1), jnp.swapaxes(bc_new, 0, 1), jnp.swapaxes(dt_new, 0, 1))
    state_out, tail_x_out, tail_bc_out, y_slots = lax.map(per_slot, slot_inputs)
    return (state_out, tail_x_out, tail_bc_out, jnp.swapaxes(y_slots, 0, 1))
```

```python
import functools
import jax
import jax.numpy as jnp
from jax import lax
from jax.experimental import pallas as pl
from jax.experimental.pallas import tpu as pltpu
from jax.sharding import PartitionSpec as P

STEPS = 2
EPSILON = 1e-05
MESH = pl.DeviceIdType.MESH
CHUNKS = 2
TAIL_ROWS = 2


def partner_of(me, i, devices):
    return lax.rem(me + i, devices)


def relocate_kernel(
    devices,
    heads,
    source,
    state_hbm,
    tail_x,
    tail_bc,
    moved,
    tails_out,
    state,
    tails,
    first_a,
    first_b,
    spread_a,
    spread_b,
    second_a,
    second_b,
    back_a,
    back_b,
    load_sem,
    send_sem,
    recv_sem,
):
    me = lax.axis_index("rows")
    part = heads // CHUNKS
    lanes = 128
    first, spread, second, back = (
        (first_a, first_b),
        (spread_a, spread_b),
        (second_a, second_b),
        (back_a, back_b),
    )
    load = pltpu.make_async_copy(state_hbm, state, load_sem)
    load.start()
    barrier = pltpu.get_barrier_semaphore()

    def greet(i, carry):
        pl.semaphore_signal(
            barrier,
            inc=1,
            device_id={"rows": partner_of(me, i, devices)},
            device_id_type=MESH,
        )
        return carry

    lax.fori_loop(1, devices, greet, 0)

    low = source[2 * me]
    high = source[2 * me + 1]
    given = jnp.where((low != 2 * me) & (high != 2 * me), 0, 1)

    for k in range(3):
        tails[16 * k : 16 * k + 16, :] = tail_x[given, k].astype(jnp.float32)
        for b in range(2):
            entry = tail_bc[given, k, b].astype(jnp.float32)
            at = 48 + (2 * k + b) * 8
            tails[at : at + 4, :] = entry[:, :lanes]
            tails[at + 4 : at + 8, :] = entry[:, lanes:]

    def remote(phase, chunk, to):
        source_ref, target_ref = ((first, spread), (second, back))[phase]
        return pltpu.make_async_remote_copy(
            src_ref=source_ref[chunk].at[to],
            dst_ref=target_ref[chunk].at[me],
            send_sem=send_sem.at[phase, chunk],
            recv_sem=recv_sem.at[phase, chunk],
            device_id={"rows": to},
            device_id_type=MESH,
        )

    def all_pieces(phase, chunk):
        source_ref, target_ref = ((first, spread), (second, back))[phase]
        return pltpu.make_async_remote_copy(
            src_ref=source_ref[chunk].at[pl.ds(0, devices - 1)],
            dst_ref=target_ref[chunk].at[pl.ds(0, devices - 1)],
            send_sem=send_sem.at[phase, chunk],
            recv_sem=recv_sem.at[phase, chunk],
            device_id={"rows": partner_of(me, 1, devices)},
            device_id_type=MESH,
        )

    def pack(chunk, piece, into, at):
        rows = state[given, piece, chunk * part : (chunk + 1) * part, :]
        into[at, 0:part, :] = rows[:, :lanes]
        into[at, part : 2 * part, :] = rows[:, lanes:]
        if chunk == 0:
            into[at, 2 * part, :] = tails[piece, :]
            into[at, 2 * part + 1, :] = tails[64 + lax.rem(piece, 32), :]

    load.wait()
    pl.semaphore_wait(barrier, devices - 1)
    for chunk in range(CHUNKS):

        def begin(i, carry, chunk=chunk):
            to = partner_of(me, i, devices)
            pack(chunk, to, first[chunk], to)
            remote(0, chunk, to).start()
            return carry

        lax.fori_loop(1, devices, begin, 0)
        pack(chunk, me, spread[chunk], me)

    def giver(to):
        from_low = lax.shift_right_logical(source[2 * to], 1)
        from_high = lax.shift_right_logical(source[2 * to + 1], 1)
        return jnp.where(from_low != to, from_low, from_high)

    for chunk in range(CHUNKS):
        all_pieces(0, chunk).wait_recv()

        def forward(i, carry, chunk=chunk):
            to = partner_of(me, i, devices)
            second[chunk][to] = spread[chunk][giver(to)]
            remote(1, chunk, to).start()
            return carry

        lax.fori_loop(1, devices, forward, 0)
        back[chunk][me] = spread[chunk][giver(me)]

    for chunk in range(CHUNKS):
        all_pieces(1, chunk).wait_recv()

        def unpack(k, carry, chunk=chunk):
            moved[k, chunk * part : (chunk + 1) * part, 0:lanes] = back[chunk][k, 0:part, :]
            moved[k, chunk * part : (chunk + 1) * part, lanes:] = back[chunk][
                k, part : 2 * part, :
            ]
            if chunk == 0:
                tails_out[64 + lax.rem(k, 32), :] = back[0][k, 2 * part + 1, :]
                tails_out[k, :] = back[0][k, 2 * part, :]
            return carry

        lax.fori_loop(0, devices, unpack, 0)

    for phase in range(2):
        for chunk in range(CHUNKS):
            all_pieces(phase, chunk).wait_send()


def relocate(state_in, tail_x, tail_bc, source):
    devices = lax.axis_size("rows")
    slots, depth, head_count, width = state_in.shape
    heads = depth * head_count // devices
    part = heads // CHUNKS
    pieces = state_in.reshape(slots, devices, heads, width)
    long_buffer = pltpu.VMEM((devices, 2 * part + TAIL_ROWS, 128), jnp.float32)
    short_buffer = pltpu.VMEM((devices, 2 * part, 128), jnp.float32)
    vmem = pl.BlockSpec(memory_space=pltpu.VMEM)
    moved, tails = pl.pallas_call(
        functools.partial(relocate_kernel, devices, heads),
        out_shape=(
            jax.ShapeDtypeStruct((devices, heads, width), jnp.float32),
            jax.ShapeDtypeStruct((96, 128), jnp.float32),
        ),
        in_specs=[
            pl.BlockSpec(memory_space=pltpu.SMEM),
            pl.BlockSpec(memory_space=pl.ANY),
            vmem,
            vmem,
        ],
        out_specs=(vmem, vmem),
        scratch_shapes=[
            pltpu.VMEM((slots, devices, heads, width), jnp.float32),
            pltpu.VMEM((96, 128), jnp.float32),
        ]
        + [long_buffer, short_buffer] * 4
        + [
            pltpu.SemaphoreType.DMA,
            pltpu.SemaphoreType.DMA((2, CHUNKS)),
            pltpu.SemaphoreType.DMA((2, CHUNKS)),
        ],
        compiler_params=pltpu.CompilerParams(
            collective_id=0, has_side_effects=True, vmem_limit_bytes=48 * 1024 * 1024
        ),
    )(source, pieces, tail_x, tail_bc)
    me = lax.axis_index("rows")
    mine = lax.dynamic_slice(source, (2 * me,), (2,))
    local = mine - 2 * me
    here = (local >= 0) & (local < slots)
    safe = jnp.clip(local, 0, slots - 1)
    moved = moved.reshape(depth, head_count, width)
    moved_x = tails[:48].reshape(3, depth, head_count).astype(jnp.bfloat16)
    halves = tails[48:].reshape(3, 2, 2, 4, 128)
    moved_bc = jnp.transpose(halves, (0, 1, 3, 2, 4)).reshape(3, 2, 4, 256).astype(jnp.bfloat16)

    def pick(array, new):
        swapped = jnp.where(
            (safe == 0).reshape((2,) + (1,) * new.ndim), array[0][None], array[1][None]
        )
        return jnp.where(here.reshape((2,) + (1,) * new.ndim), swapped, new[None])

    return pick(state_in, moved), pick(tail_x, moved_x), pick(tail_bc, moved_bc)


def on_device(
    state_in,
    tail_x,
    tail_bc,
    source,
    active,
    x_new,
    z_new,
    bc_new,
    dt_new,
    conv_wx,
    conv_bx,
    conv_wbc,
    conv_bbc,
    dt_bias,
    a_log,
    skip_d,
    norm_gain,
):
    state, window_x, window_bc = relocate(state_in, tail_x, tail_bc, source)
    slot_count, depth_dev, head_count, state_width = state.shape
    groups = conv_wbc.shape[2]
    per_group = head_count // groups
    full_depth = depth_dev * lax.axis_size("tp")
    live = active == 1
    live_state = live[:, None, None, None]
    live_bc = live[:, None, None, None, None]
    rate = jnp.exp(a_log)
    outputs = []
    for step_index in range(STEPS):
        entry_x = x_new[step_index]
        entry_bc = bc_new[step_index]
        frame_x = jnp.concatenate([window_x, entry_x[:, None]], axis=1).astype(jnp.float32)
        conv_x = jax.nn.silu(jnp.sum(frame_x * conv_wx[None], axis=1) + conv_bx)
        frame_bc = jnp.concatenate([window_bc, entry_bc[:, None]], axis=1).astype(jnp.float32)
        conv_bc = jax.nn.silu(jnp.sum(frame_bc * conv_wbc[None], axis=1) + conv_bbc)
        expand_b = jnp.repeat(conv_bc[:, 0], per_group, axis=1)
        expand_c = jnp.repeat(conv_bc[:, 1], per_group, axis=1)
        step_size = jax.nn.softplus(dt_new[step_index] + dt_bias)
        decay = jnp.exp(-step_size * rate)
        candidate = (
            state * decay[:, None, :, None]
            + (step_size[:, None, :] * conv_x)[..., None] * expand_b[:, None]
        )
        readout = jnp.sum(candidate * expand_c[:, None], axis=-1) + skip_d * conv_x
        gated = readout * jax.nn.silu(z_new[step_index].astype(jnp.float32))
        totals = lax.psum(
            jnp.sum(
                jnp.square(gated).reshape(slot_count, depth_dev, groups, per_group), axis=(1, 3)
            ),
            "tp",
        )
        factor = lax.rsqrt(totals / (full_depth * per_group) + EPSILON)
        scaled = gated * jnp.repeat(factor, per_group, axis=1)[:, None, :] * norm_gain
        outputs.append(jnp.where(live[:, None, None], scaled, 0.0).astype(jnp.bfloat16))
        state = jnp.where(live_state, candidate, state)
        window_x = jnp.where(
            live_state, jnp.concatenate([window_x[:, 1:], entry_x[:, None]], axis=1), window_x
        )
        window_bc = jnp.where(
            live_bc, jnp.concatenate([window_bc[:, 1:], entry_bc[:, None]], axis=1), window_bc
        )
    return (state, window_x, window_bc, jnp.stack(outputs))


def solution(mesh):
    return jax.shard_map(
        on_device,
        mesh=mesh,
        in_specs=(
            P("rows", "tp", None, None),
            P("rows", None, "tp", None),
            P("rows", None, None, None, None),
            P(),
            P("rows"),
            P(None, "rows", "tp", None),
            P(None, "rows", "tp", None),
            P(None, "rows", None, None, None),
            P(None, "rows", None),
            P(None, "tp", None),
            P("tp", None),
            P(),
            P(),
            P(),
            P(),
            P(),
            P("tp", None),
        ),
        out_specs=(
            P("rows", "tp", None, None),
            P("rows", None, "tp", None),
            P("rows", None, None, None, None),
            P(None, "rows", "tp", None),
        ),
        check_vma=False,
    )
```

```python
import functools
import jax
import jax.numpy as jnp
from jax import lax
from jax.experimental import pallas as pl
from jax.experimental.pallas import tpu as pltpu
from jax.sharding import PartitionSpec as P

STEPS = 2
EPSILON = 1e-05
MESH = pl.DeviceIdType.MESH
CHUNKS = 2
TAIL_ROWS = 2
LANES = 128
DEPTH = 16
GROUPS = 4
PER_GROUP = 32
PART = PER_GROUP // CHUNKS
TP = 4

COEF = 0
INPUT_B = 256
Y_ROWS = 288
TAIL_X = 352
TAIL_BC = 448
PACK_ROWS = 544


def silu(v):
    return v / (1.0 + jnp.exp(-v))


def partner_of(me, i, devices):
    return lax.rem(me + i, devices)


def given_of(low, high, me):
    return jnp.where((low != 2 * me) & (high != 2 * me), 0, 1)


def relocate_kernel(
    devices,
    source_hbm,
    active_hbm,
    state_hbm,
    tail_x_hbm,
    tail_bc_hbm,
    x_new_hbm,
    z_new_hbm,
    bc_new_hbm,
    dt_new_hbm,
    conv_wx_hbm,
    conv_bx_hbm,
    conv_wbc_hbm,
    conv_bbc_hbm,
    dt_bias_hbm,
    a_log_hbm,
    skip_d_hbm,
    norm_gain_hbm,
    moved_a,
    moved_b,
    pack_hbm,
    source,
    active,
    state,
    tail_x,
    tail_bc,
    x_new,
    z_new,
    bc_new,
    dt_new,
    conv_wx,
    conv_bx,
    conv_wbc,
    conv_bbc,
    dt_bias,
    a_log,
    skip_d,
    norm_gain,
    tails,
    first_a,
    first_b,
    spread_a,
    spread_b,
    second_a,
    second_b,
    back_a,
    back_b,
    pack,
    rows_c,
    decays,
    extras,
    gates,
    dots,
    turned,
    sums,
    sums_in,
    load_sem,
    send_sem,
    recv_sem,
    sum_send_sem,
    sum_recv_sem,
    out_sem,
):
    me = lax.axis_index("rows")
    column = lax.axis_index("tp")
    first, spread, second, back = (
        (first_a, first_b),
        (spread_a, spread_b),
        (second_a, second_b),
        (back_a, back_b),
    )
    loads = [
        pltpu.make_async_copy(src, dst, load_sem.at[i])
        for i, (src, dst) in enumerate(
            (
                (source_hbm, source),
                (tail_x_hbm, tail_x),
                (tail_bc_hbm, tail_bc),
                (state_hbm, state),
                (active_hbm, active),
                (x_new_hbm, x_new),
                (z_new_hbm, z_new),
                (bc_new_hbm, bc_new),
                (dt_new_hbm, dt_new),
                (conv_wx_hbm, conv_wx),
                (conv_bx_hbm, conv_bx),
                (conv_wbc_hbm, conv_wbc),
                (conv_bbc_hbm, conv_bbc),
                (dt_bias_hbm, dt_bias),
                (a_log_hbm, a_log),
                (skip_d_hbm, skip_d),
                (norm_gain_hbm, norm_gain),
            )
        )
    ]
    for load in loads:
        load.start()
    barrier = pltpu.get_barrier_semaphore()

    def greet(i, carry):
        pl.semaphore_signal(
            barrier,
            inc=1,
            device_id={"rows": partner_of(me, i, devices)},
            device_id_type=MESH,
        )
        return carry

    lax.fori_loop(1, devices, greet, 0)
    for j in range(1, TP):
        pl.semaphore_signal(
            barrier,
            inc=1,
            device_id={"tp": lax.rem(column + j, TP)},
            device_id_type=MESH,
        )

    loads[0].wait()
    low = source[2 * me]
    high = source[2 * me + 1]
    given = given_of(low, high, me)
    kept = 1 - given
    kept_slot = jnp.where(low == 2 * me + kept, 0, 1)
    moved_slot = 1 - kept_slot

    loads[1].wait()
    loads[2].wait()
    for k in range(3):
        tails[DEPTH * k : DEPTH * (k + 1), :] = tail_x[given, k].astype(jnp.float32)
        for b in range(2):
            entry = tail_bc[given, k, b].astype(jnp.float32)
            at = 48 + (2 * k + b) * 8
            tails[at : at + 4, :] = entry[:, :LANES]
            tails[at + 4 : at + 8, :] = entry[:, LANES:]

    def remote(phase, chunk, to):
        source_ref, target_ref = ((first, spread), (second, back))[phase]
        return pltpu.make_async_remote_copy(
            src_ref=source_ref[chunk].at[to],
            dst_ref=target_ref[chunk].at[me],
            send_sem=send_sem.at[phase, chunk],
            recv_sem=recv_sem.at[phase, chunk],
            device_id={"rows": to},
            device_id_type=MESH,
        )

    def all_pieces(phase, chunk):
        source_ref, target_ref = ((first, spread), (second, back))[phase]
        return pltpu.make_async_remote_copy(
            src_ref=source_ref[chunk].at[pl.ds(0, devices - 1)],
            dst_ref=target_ref[chunk].at[pl.ds(0, devices - 1)],
            send_sem=send_sem.at[phase, chunk],
            recv_sem=recv_sem.at[phase, chunk],
            device_id={"rows": partner_of(me, 1, devices)},
            device_id_type=MESH,
        )

    def fill(chunk, piece, into, at):
        rows = state[given, piece, chunk * PART : (chunk + 1) * PART, :]
        into[at, 0:PART, :] = rows[:, :LANES]
        into[at, PART : 2 * PART, :] = rows[:, LANES:]
        if chunk == 0:
            into[at, 2 * PART, :] = tails[piece, :]
            into[at, 2 * PART + 1, :] = tails[64 + lax.rem(piece, 32), :]

    loads[3].wait()
    pl.semaphore_wait(barrier, devices - 1 + TP - 1)
    for chunk in range(CHUNKS):

        def begin(i, carry, chunk=chunk):
            to = partner_of(me, i, devices)
            fill(chunk, to, first[chunk], to)
            remote(0, chunk, to).start()
            return carry

        lax.fori_loop(1, devices, begin, 0)
        fill(chunk, me, spread[chunk], me)

    for load in loads[4:]:
        load.wait()
    group_of_lane = lax.broadcasted_iota(jnp.int32, (GROUPS, LANES), 1) // PER_GROUP
    own_group = group_of_lane == lax.broadcasted_iota(jnp.int32, (GROUPS, LANES), 0)
    lane = lax.broadcasted_iota(jnp.int32, (8, LANES), 1)

    def by_head(values):
        return jnp.sum(jnp.where(own_group, values, 0.0), axis=0, keepdims=True)

    def prepare(row, slot, window_x, window_bc):
        live = active[slot] == 1
        new_x = [x_new[s, slot].astype(jnp.float32) for s in range(STEPS)]
        new_bc = [
            [bc_new[s, slot, b].astype(jnp.float32) for b in range(2)] for s in range(STEPS)
        ]
        frames_x = window_x + new_x
        frames_bc = window_bc + new_bc
        conv_x = []
        conv_b = []
        conv_c = []
        sizes = []
        decay = []
        rate = jnp.exp(a_log[...])
        for s in range(STEPS):
            total = frames_x[s] * conv_wx[0]
            for k in range(1, 4):
                total = total + frames_x[s + k] * conv_wx[k]
            conv_x.append(silu(total + conv_bx[...]))
            pair = []
            for b in range(2):
                total = frames_bc[s][b] * conv_wbc[0, b]
                for k in range(1, 4):
                    total = total + frames_bc[s + k][b] * conv_wbc[k, b]
                pair.append(silu(total + conv_bbc[b]))
            conv_b.append(pair[0])
            conv_c.append(pair[1])
            raw = jnp.where(slot == 0, dt_new[s, 0:1, :], dt_new[s, 1:2, :]) + dt_bias[...]
            size = jnp.maximum(raw, 0.0) + jnp.log1p(jnp.exp(-jnp.abs(raw)))
            sizes.append(size)
            decay.append(jnp.exp(-size * rate))
            for half in range(2):
                for g in range(GROUPS):
                    rows_c[row, s, half, g] = jnp.broadcast_to(
                        pair[1][g : g + 1, half * LANES : (half + 1) * LANES], (8, LANES)
                    )
            at = INPUT_B + (row * STEPS + s) * 8
            pack[at : at + 4, :] = pair[0][:, :LANES]
            pack[at + 4 : at + 8, :] = pair[0][:, LANES:]
            gates[row, s] = silu(z_new[s, slot].astype(jnp.float32))

        def overlap(i, j):
            return by_head(jnp.sum(conv_b[i] * conv_c[j], axis=1, keepdims=True))

        skip = skip_d[...]
        put_in = [sizes[s] * conv_x[s] for s in range(STEPS)]
        carried = put_in[0] * decay[1]
        both = decay[0] * decay[1]
        decays[row, 0] = jnp.broadcast_to(decay[0], (DEPTH, LANES))
        decays[row, 1] = jnp.broadcast_to(both, (DEPTH, LANES))
        extras[row, 0] = put_in[0] * overlap(0, 0) + skip * conv_x[0]
        extras[row, 1] = (
            carried * overlap(0, 1) + put_in[1] * overlap(1, 1) + skip * conv_x[1]
        )
        turned[0:DEPTH, :] = jnp.where(live, carried, 0.0)
        turned[DEPTH : 2 * DEPTH, :] = jnp.where(live, put_in[1], 0.0)
        turned[2 * DEPTH : 2 * DEPTH + 8, :] = jnp.broadcast_to(
            jnp.where(live, both, 1.0), (8, LANES)
        )
        turned[2 * DEPTH + 8 :, :] = jnp.zeros((LANES - 2 * DEPTH - 8, LANES), jnp.float32)
        at = COEF + row * LANES
        pack[at : at + LANES, :] = jnp.transpose(turned[...])
        for k in range(3):
            at = TAIL_X + (row * 3 + k) * DEPTH
            pack[at : at + DEPTH, :] = jnp.where(live, frames_x[k + 2], frames_x[k])
            for b in range(2):
                entry = jnp.where(live, frames_bc[k + 2][b], frames_bc[k][b])
                at = TAIL_BC + ((row * 3 + k) * 2 + b) * 8
                pack[at : at + 4, :] = entry[:, :LANES]
                pack[at + 4 : at + 8, :] = entry[:, LANES:]

    def readout(row, octets, piece):
        def one_group(g, carry):
            c = [
                [rows_c[row, s, half, g] for half in range(2)] for s in range(STEPS)
            ]
            for octet in octets:
                held = [jnp.zeros((8, LANES), jnp.float32) for _ in range(STEPS)]
                for p in range(DEPTH):
                    left, right = piece(GROUPS * p + g, octet)
                    for s in range(STEPS):
                        dot = jnp.sum(
                            left * c[s][0] + right * c[s][1], axis=1, keepdims=True
                        )
                        held[s] = jnp.where(lane == p, dot, held[s])
                for s in range(STEPS):
                    at = pl.multiple_of(g * PER_GROUP + octet * 8, 8)
                    dots[s, pl.ds(at, 8), :] = held[s]
            return carry

        lax.fori_loop(0, GROUPS, one_group, 0)

    def finish(row):
        for s in range(STEPS):
            dot = jnp.transpose(dots[s])[0:DEPTH, :]
            gated = (decays[row, s] * dot + extras[row, s]) * gates[row, s]
            gates[row, s] = gated
            sums[row * STEPS + s : row * STEPS + s + 1, :] = jnp.sum(
                gated * gated, axis=0, keepdims=True
            )

    prepare(
        0,
        kept_slot,
        [tail_x[kept, k].astype(jnp.float32) for k in range(3)],
        [[tail_bc[kept, k, b].astype(jnp.float32) for b in range(2)] for k in range(3)],
    )
    sums[4:8, :] = jnp.zeros((4, LANES), jnp.float32)

    def kept_piece(at, octet):
        rows = state[kept, at, 8 * octet : 8 * octet + 8, :]
        return rows[:, :LANES], rows[:, LANES:]

    readout(0, range(PER_GROUP // 8), kept_piece)
    finish(0)

    def giver(to):
        from_low = lax.shift_right_logical(source[2 * to], 1)
        from_high = lax.shift_right_logical(source[2 * to + 1], 1)
        return jnp.where(from_low != to, from_low, from_high)

    for chunk in range(CHUNKS):
        all_pieces(0, chunk).wait_recv()

        def forward(i, carry, chunk=chunk):
            to = partner_of(me, i, devices)
            second[chunk][to] = spread[chunk][giver(to)]
            remote(1, chunk, to).start()
            return carry

        lax.fori_loop(1, devices, forward, 0)
        back[chunk][me] = spread[chunk][giver(me)]

    outs = [
        pltpu.make_async_copy(back_a, moved_a, out_sem.at[0]),
        pltpu.make_async_copy(back_b, moved_b, out_sem.at[1]),
        pltpu.make_async_copy(pack, pack_hbm, out_sem.at[2]),
    ]
    for chunk in range(CHUNKS):
        all_pieces(1, chunk).wait_recv()
        outs[chunk].start()
        if chunk == 0:

            def untail(k, carry):
                tails[64 + lax.rem(k, 32), :] = back_a[k, 2 * PART + 1, :]
                tails[k, :] = back_a[k, 2 * PART, :]
                return carry

            lax.fori_loop(0, devices, untail, 0)
            window_bc = [
                [
                    jnp.concatenate(
                        [
                            tails[48 + (2 * k + b) * 8 : 52 + (2 * k + b) * 8, :],
                            tails[52 + (2 * k + b) * 8 : 56 + (2 * k + b) * 8, :],
                        ],
                        axis=1,
                    )
                    for b in range(2)
                ]
                for k in range(3)
            ]
            prepare(
                1,
                moved_slot,
                [tails[DEPTH * k : DEPTH * (k + 1), :] for k in range(3)],
                window_bc,
            )

        def moved_piece(at, octet, chunk=chunk):
            within = 8 * octet - PART * chunk
            return (
                back[chunk][at, within : within + 8, :],
                back[chunk][at, PART + within : PART + within + 8, :],
            )

        readout(1, range(chunk * PART // 8, (chunk + 1) * PART // 8), moved_piece)
    finish(1)

    exchanges = [
        pltpu.make_async_remote_copy(
            src_ref=sums,
            dst_ref=sums_in.at[j - 1],
            send_sem=sum_send_sem.at[j - 1],
            recv_sem=sum_recv_sem.at[j - 1],
            device_id={"tp": lax.rem(column + j, TP)},
            device_id_type=MESH,
        )
        for j in range(1, TP)
    ]
    for exchange in exchanges:
        exchange.start()
    same_group = (
        lax.broadcasted_iota(jnp.int32, (LANES, LANES), 0) // PER_GROUP
        == lax.broadcasted_iota(jnp.int32, (LANES, LANES), 1) // PER_GROUP
    ).astype(jnp.float32)
    for exchange in exchanges:
        exchange.wait_recv()
    totals = jnp.dot(
        sums[...] + sums_in[0] + sums_in[1] + sums_in[2],
        same_group,
        preferred_element_type=jnp.float32,
        precision=lax.Precision.HIGHEST,
    )
    factor = lax.rsqrt(totals / (DEPTH * TP * PER_GROUP) + EPSILON)
    for row in range(2):
        live = active[jnp.where(row == 0, kept_slot, moved_slot)] == 1
        for s in range(STEPS):
            scale = factor[row * STEPS + s : row * STEPS + s + 1, :]
            at = Y_ROWS + (row * STEPS + s) * DEPTH
            pack[at : at + DEPTH, :] = jnp.where(
                live, gates[row, s] * scale * norm_gain[...], 0.0
            )
    outs[2].start()
    for exchange in exchanges:
        exchange.wait_send()
    for phase in range(2):
        for chunk in range(CHUNKS):
            all_pieces(phase, chunk).wait_send()
    for out in outs:
        out.wait()


QUARTERS = 4


def state_kernel(
    devices,
    source_hbm,
    state_hbm,
    moved_a_hbm,
    moved_b_hbm,
    pack_hbm,
    state_out,
    tail_x_out,
    tail_bc_out,
    y_out,
    source,
    kept_in,
    moved_a,
    moved_b,
    pack,
    result,
    tail_x,
    tail_bc,
    y,
    sem,
    part_sem,
):
    me = lax.axis_index("rows")
    size = devices // QUARTERS

    def piece_range(q):
        return pl.ds(q * size, size)

    source_load = pltpu.make_async_copy(source_hbm, source, sem.at[0])
    pack_load = pltpu.make_async_copy(pack_hbm, pack, sem.at[1])
    source_load.start()
    pack_load.start()
    moved_loads = [
        [
            pltpu.make_async_copy(
                hbm.at[piece_range(q)], vmem.at[piece_range(q)], part_sem.at[c, q]
            )
            for c, (hbm, vmem) in enumerate(((moved_a_hbm, moved_a), (moved_b_hbm, moved_b)))
        ]
        for q in range(QUARTERS)
    ]
    for pair in moved_loads:
        for load in pair:
            load.start()
    source_load.wait()
    low = source[2 * me]
    high = source[2 * me + 1]
    kept = 1 - given_of(low, high, me)
    kept_slot = jnp.where(low == 2 * me + kept, 0, 1)
    slots = (kept_slot, 1 - kept_slot)
    kept_loads = [
        pltpu.make_async_copy(
            state_hbm.at[kept, piece_range(q)], kept_in.at[piece_range(q)], part_sem.at[2, q]
        )
        for q in range(QUARTERS)
    ]
    for load in kept_loads:
        load.start()
    pack_load.wait()
    writes = []
    for row in (1, 0):
        base = COEF + row * LANES
        b = [
            pack[
                INPUT_B + (row * STEPS + s) * 8 : INPUT_B + (row * STEPS + s) * 8 + 8, :
            ]
            for s in range(STEPS)
        ]
        for q in range(QUARTERS):
            if row == 1:
                for load in moved_loads[q]:
                    load.wait()
            else:
                kept_loads[q].wait()
            for p in range(q * DEPTH // QUARTERS, (q + 1) * DEPTH // QUARTERS):
                for g in range(GROUPS):
                    k = GROUPS * p + g
                    for octet in range(PER_GROUP // 8):
                        head = base + g * PER_GROUP + octet * 8
                        u1 = pack[head : head + 8, p : p + 1]
                        u2 = pack[head : head + 8, DEPTH + p : DEPTH + p + 1]
                        decay = pack[head : head + 8, 2 * DEPTH : 2 * DEPTH + 1]
                        for half in range(2):
                            if row == 1:
                                chunk = octet * 8 // PART
                                at = half * PART + octet * 8 - chunk * PART
                                held = (moved_a, moved_b)[chunk][k, at : at + 8, :]
                            else:
                                held = kept_in[
                                    k,
                                    octet * 8 : octet * 8 + 8,
                                    half * LANES : (half + 1) * LANES,
                                ]
                            at = half * GROUPS + g
                            result[
                                row,
                                k,
                                octet * 8 : octet * 8 + 8,
                                half * LANES : (half + 1) * LANES,
                            ] = (
                                held * decay + u1 * b[0][at : at + 1, :] + u2 * b[1][at : at + 1, :]
                            )
            write = pltpu.make_async_copy(
                result.at[row, piece_range(q)],
                state_out.at[slots[row], piece_range(q)],
                part_sem.at[3 + row, q],
            )
            write.start()
            writes.append(write)
        slot = slots[row]
        for s in range(STEPS):
            at = Y_ROWS + (row * STEPS + s) * DEPTH
            y[s, slot] = pack[at : at + DEPTH, :].astype(jnp.bfloat16)
        for k in range(3):
            at = TAIL_X + (row * 3 + k) * DEPTH
            tail_x[slot, k] = pack[at : at + DEPTH, :].astype(jnp.bfloat16)
            for c in range(2):
                at = TAIL_BC + ((row * 3 + k) * 2 + c) * 8
                tail_bc[slot, k, c] = jnp.concatenate(
                    [pack[at : at + 4, :], pack[at + 4 : at + 8, :]], axis=1
                ).astype(jnp.bfloat16)
    for i, (vmem, hbm) in enumerate(((tail_x, tail_x_out), (tail_bc, tail_bc_out), (y, y_out))):
        write = pltpu.make_async_copy(vmem, hbm, sem.at[2 + i])
        write.start()
        writes.append(write)
    for write in writes:
        write.wait()


def on_device(
    state_in,
    tail_x,
    tail_bc,
    source,
    active,
    x_new,
    z_new,
    bc_new,
    dt_new,
    conv_wx,
    conv_bx,
    conv_wbc,
    conv_bbc,
    dt_bias,
    a_log,
    skip_d,
    norm_gain,
):
    devices = lax.axis_size("rows")
    slots, depth, head_count, width = state_in.shape
    pieces = state_in.reshape(slots, devices, PER_GROUP, width)
    operands = (
        source,
        active,
        pieces,
        tail_x,
        tail_bc,
        x_new,
        z_new,
        bc_new,
        dt_new,
        conv_wx,
        conv_bx,
        conv_wbc,
        conv_bbc,
        dt_bias.reshape(1, -1),
        a_log.reshape(1, -1),
        skip_d.reshape(1, -1),
        norm_gain,
    )
    long_buffer = pltpu.VMEM((devices, 2 * PART + TAIL_ROWS, LANES), jnp.float32)
    short_buffer = pltpu.VMEM((devices, 2 * PART, LANES), jnp.float32)
    hbm = pl.BlockSpec(memory_space=pltpu.HBM)
    moved_a, moved_b, pack = pl.pallas_call(
        functools.partial(relocate_kernel, devices),
        out_shape=(
            jax.ShapeDtypeStruct(long_buffer.shape, jnp.float32),
            jax.ShapeDtypeStruct(short_buffer.shape, jnp.float32),
            jax.ShapeDtypeStruct((PACK_ROWS, LANES), jnp.float32),
        ),
        in_specs=[hbm] * len(operands),
        out_specs=(hbm, hbm, hbm),
        scratch_shapes=[
            pltpu.SMEM(source.shape, jnp.int32),
            pltpu.SMEM(active.shape, jnp.int32),
        ]
        + [pltpu.VMEM(a.shape, a.dtype) for a in operands[2:]]
        + [pltpu.VMEM((96, LANES), jnp.float32)]
        + [long_buffer, short_buffer] * 4
        + [
            pltpu.VMEM((PACK_ROWS, LANES), jnp.float32),
            pltpu.VMEM((2, STEPS, 2, GROUPS, 8, LANES), jnp.float32),
            pltpu.VMEM((2, STEPS, DEPTH, LANES), jnp.float32),
            pltpu.VMEM((2, STEPS, DEPTH, LANES), jnp.float32),
            pltpu.VMEM((2, STEPS, DEPTH, LANES), jnp.float32),
            pltpu.VMEM((STEPS, LANES, LANES), jnp.float32),
            pltpu.VMEM((LANES, LANES), jnp.float32),
            pltpu.VMEM((8, LANES), jnp.float32),
            pltpu.VMEM((TP - 1, 8, LANES), jnp.float32),
            pltpu.SemaphoreType.DMA((len(operands),)),
            pltpu.SemaphoreType.DMA((2, CHUNKS)),
            pltpu.SemaphoreType.DMA((2, CHUNKS)),
            pltpu.SemaphoreType.DMA((TP - 1,)),
            pltpu.SemaphoreType.DMA((TP - 1,)),
            pltpu.SemaphoreType.DMA((3,)),
        ],
        compiler_params=pltpu.CompilerParams(
            collective_id=0, has_side_effects=True, vmem_limit_bytes=48 * 1024 * 1024
        ),
    )(*operands)
    state, window_x, window_bc, y = pl.pallas_call(
        functools.partial(state_kernel, devices),
        out_shape=(
            jax.ShapeDtypeStruct(pieces.shape, jnp.float32),
            jax.ShapeDtypeStruct(tail_x.shape, tail_x.dtype),
            jax.ShapeDtypeStruct(tail_bc.shape, tail_bc.dtype),
            jax.ShapeDtypeStruct(x_new.shape, jnp.bfloat16),
        ),
        in_specs=[hbm] * 5,
        out_specs=(hbm,) * 4,
        scratch_shapes=[
            pltpu.SMEM(source.shape, jnp.int32),
            pltpu.VMEM((devices, PER_GROUP, width), jnp.float32),
            long_buffer,
            short_buffer,
            pltpu.VMEM((PACK_ROWS, LANES), jnp.float32),
            pltpu.VMEM(pieces.shape, jnp.float32),
            pltpu.VMEM(tail_x.shape, tail_x.dtype),
            pltpu.VMEM(tail_bc.shape, tail_bc.dtype),
            pltpu.VMEM(x_new.shape, jnp.bfloat16),
            pltpu.SemaphoreType.DMA((5,)),
            pltpu.SemaphoreType.DMA((5, QUARTERS)),
        ],
        compiler_params=pltpu.CompilerParams(vmem_limit_bytes=48 * 1024 * 1024),
    )(source, pieces, moved_a, moved_b, pack)
    return state.reshape(state_in.shape), window_x, window_bc, y


def solution(mesh):
    return jax.shard_map(
        on_device,
        mesh=mesh,
        in_specs=(
            P("rows", "tp", None, None),
            P("rows", None, "tp", None),
            P("rows", None, None, None, None),
            P(),
            P("rows"),
            P(None, "rows", "tp", None),
            P(None, "rows", "tp", None),
            P(None, "rows", None, None, None),
            P(None, "rows", None),
            P(None, "tp", None),
            P("tp", None),
            P(),
            P(),
            P(),
            P(),
            P(),
            P("tp", None),
        ),
        out_specs=(
            P("rows", "tp", None, None),
            P("rows", None, "tp", None),
            P("rows", None, None, None, None),
            P(None, "rows", "tp", None),
        ),
        check_vma=False,
    )
```

```python
import functools
import jax
import jax.numpy as jnp
from jax import lax
from jax.experimental import pallas as pl
from jax.experimental.pallas import tpu as pltpu
from jax.sharding import PartitionSpec as P

STEPS = 2
EPSILON = 1e-05
MESH = pl.DeviceIdType.MESH
CHUNKS = 2
TAIL_ROWS = 2
LANES = 128
DEPTH = 16
GROUPS = 4
PER_GROUP = 32
PART = PER_GROUP // CHUNKS
TP = 4

COEF = 0
INPUT_B = 256
Y_ROWS = 288
TAIL_X = 352
TAIL_BC = 448
PACK_ROWS = 544


def silu(v):
    return v / (1.0 + jnp.exp(-v))


def partner_of(me, i, devices):
    return lax.rem(me + i, devices)


def given_of(low, high, me):
    return jnp.where((low != 2 * me) & (high != 2 * me), 0, 1)


def relocate_kernel(
    devices,
    source_hbm,
    active_hbm,
    state_hbm,
    tail_x_hbm,
    tail_bc_hbm,
    x_new_hbm,
    z_new_hbm,
    bc_new_hbm,
    dt_new_hbm,
    conv_wx_hbm,
    conv_bx_hbm,
    conv_wbc_hbm,
    conv_bbc_hbm,
    dt_bias_hbm,
    a_log_hbm,
    skip_d_hbm,
    norm_gain_hbm,
    moved_a,
    moved_b,
    pack_hbm,
    source,
    active,
    state,
    tail_x,
    tail_bc,
    x_new,
    z_new,
    bc_new,
    dt_new,
    conv_wx,
    conv_bx,
    conv_wbc,
    conv_bbc,
    dt_bias,
    a_log,
    skip_d,
    norm_gain,
    tails,
    first_a,
    first_b,
    spread_a,
    spread_b,
    second_a,
    second_b,
    back_a,
    back_b,
    pack,
    rows_c,
    decays,
    extras,
    gates,
    dots,
    turned,
    sums,
    sums_in,
    load_sem,
    send_sem,
    recv_sem,
    sum_send_sem,
    sum_recv_sem,
    out_sem,
):
    me = lax.axis_index("rows")
    column = lax.axis_index("tp")
    first, spread, second, back = (
        (first_a, first_b),
        (spread_a, spread_b),
        (second_a, second_b),
        (back_a, back_b),
    )
    loads = [
        pltpu.make_async_copy(src, dst, load_sem.at[i])
        for i, (src, dst) in enumerate(
            (
                (source_hbm, source),
                (tail_x_hbm, tail_x),
                (tail_bc_hbm, tail_bc),
                (state_hbm, state),
                (active_hbm, active),
                (x_new_hbm, x_new),
                (z_new_hbm, z_new),
                (bc_new_hbm, bc_new),
                (dt_new_hbm, dt_new),
                (conv_wx_hbm, conv_wx),
                (conv_bx_hbm, conv_bx),
                (conv_wbc_hbm, conv_wbc),
                (conv_bbc_hbm, conv_bbc),
                (dt_bias_hbm, dt_bias),
                (a_log_hbm, a_log),
                (skip_d_hbm, skip_d),
                (norm_gain_hbm, norm_gain),
            )
        )
    ]
    for load in loads:
        load.start()
    barrier = pltpu.get_barrier_semaphore()

    def greet(i, carry):
        pl.semaphore_signal(
            barrier,
            inc=1,
            device_id={"rows": partner_of(me, i, devices)},
            device_id_type=MESH,
        )
        return carry

    lax.fori_loop(1, devices, greet, 0)
    for j in range(1, TP):
        pl.semaphore_signal(
            barrier,
            inc=1,
            device_id={"tp": lax.rem(column + j, TP)},
            device_id_type=MESH,
        )

    loads[0].wait()
    low = source[2 * me]
    high = source[2 * me + 1]
    given = given_of(low, high, me)
    kept = 1 - given
    kept_slot = jnp.where(low == 2 * me + kept, 0, 1)
    moved_slot = 1 - kept_slot

    loads[1].wait()
    loads[2].wait()
    for k in range(3):
        tails[DEPTH * k : DEPTH * (k + 1), :] = tail_x[given, k].astype(jnp.float32)
        for b in range(2):
            entry = tail_bc[given, k, b].astype(jnp.float32)
            at = 48 + (2 * k + b) * 8
            tails[at : at + 4, :] = entry[:, :LANES]
            tails[at + 4 : at + 8, :] = entry[:, LANES:]

    def remote(phase, chunk, to):
        source_ref, target_ref = ((first, spread), (second, back))[phase]
        return pltpu.make_async_remote_copy(
            src_ref=source_ref[chunk].at[to],
            dst_ref=target_ref[chunk].at[me],
            send_sem=send_sem.at[phase, chunk],
            recv_sem=recv_sem.at[phase, chunk],
            device_id={"rows": to},
            device_id_type=MESH,
        )

    def all_pieces(phase, chunk):
        source_ref, target_ref = ((first, spread), (second, back))[phase]
        return pltpu.make_async_remote_copy(
            src_ref=source_ref[chunk].at[pl.ds(0, devices - 1)],
            dst_ref=target_ref[chunk].at[pl.ds(0, devices - 1)],
            send_sem=send_sem.at[phase, chunk],
            recv_sem=recv_sem.at[phase, chunk],
            device_id={"rows": partner_of(me, 1, devices)},
            device_id_type=MESH,
        )

    def fill(chunk, piece, into, at):
        rows = state[given, piece, chunk * PART : (chunk + 1) * PART, :]
        into[at, 0:PART, :] = rows[:, :LANES]
        into[at, PART : 2 * PART, :] = rows[:, LANES:]
        if chunk == 0:
            into[at, 2 * PART, :] = tails[piece, :]
            into[at, 2 * PART + 1, :] = tails[64 + lax.rem(piece, 32), :]

    loads[3].wait()
    pl.semaphore_wait(barrier, devices - 1 + TP - 1)
    for chunk in range(CHUNKS):

        def begin(i, carry, chunk=chunk):
            to = partner_of(me, i, devices)
            fill(chunk, to, first[chunk], to)
            remote(0, chunk, to).start()
            return carry

        lax.fori_loop(1, devices, begin, 0)
        fill(chunk, me, spread[chunk], me)

    for load in loads[4:]:
        load.wait()
    group_of_lane = lax.broadcasted_iota(jnp.int32, (GROUPS, LANES), 1) // PER_GROUP
    own_group = group_of_lane == lax.broadcasted_iota(jnp.int32, (GROUPS, LANES), 0)
    lane = lax.broadcasted_iota(jnp.int32, (8, LANES), 1)

    def by_head(values):
        return jnp.sum(jnp.where(own_group, values, 0.0), axis=0, keepdims=True)

    def prepare(row, slot, window_x, window_bc):
        live = active[slot] == 1
        new_x = [x_new[s, slot].astype(jnp.float32) for s in range(STEPS)]
        new_bc = [
            [bc_new[s, slot, b].astype(jnp.float32) for b in range(2)] for s in range(STEPS)
        ]
        frames_x = window_x + new_x
        frames_bc = window_bc + new_bc
        conv_x = []
        conv_b = []
        conv_c = []
        sizes = []
        decay = []
        rate = jnp.exp(a_log[...])
        for s in range(STEPS):
            total = frames_x[s] * conv_wx[0]
            for k in range(1, 4):
                total = total + frames_x[s + k] * conv_wx[k]
            conv_x.append(silu(total + conv_bx[...]))
            pair = []
            for b in range(2):
                total = frames_bc[s][b] * conv_wbc[0, b]
                for k in range(1, 4):
                    total = total + frames_bc[s + k][b] * conv_wbc[k, b]
                pair.append(silu(total + conv_bbc[b]))
            conv_b.append(pair[0])
            conv_c.append(pair[1])
            raw = jnp.where(slot == 0, dt_new[s, 0:1, :], dt_new[s, 1:2, :]) + dt_bias[...]
            size = jnp.maximum(raw, 0.0) + jnp.log1p(jnp.exp(-jnp.abs(raw)))
            sizes.append(size)
            decay.append(jnp.exp(-size * rate))
            for half in range(2):
                for g in range(GROUPS):
                    rows_c[row, s, half, g] = jnp.broadcast_to(
                        pair[1][g : g + 1, half * LANES : (half + 1) * LANES], (8, LANES)
                    )
            at = INPUT_B + (row * STEPS + s) * 8
            pack[at : at + 4, :] = pair[0][:, :LANES]
            pack[at + 4 : at + 8, :] = pair[0][:, LANES:]
            gates[row, s] = silu(z_new[s, slot].astype(jnp.float32))

        def overlap(i, j):
            return by_head(jnp.sum(conv_b[i] * conv_c[j], axis=1, keepdims=True))

        skip = skip_d[...]
        put_in = [sizes[s] * conv_x[s] for s in range(STEPS)]
        carried = put_in[0] * decay[1]
        both = decay[0] * decay[1]
        decays[row, 0] = jnp.broadcast_to(decay[0], (DEPTH, LANES))
        decays[row, 1] = jnp.broadcast_to(both, (DEPTH, LANES))
        extras[row, 0] = put_in[0] * overlap(0, 0) + skip * conv_x[0]
        extras[row, 1] = (
            carried * overlap(0, 1) + put_in[1] * overlap(1, 1) + skip * conv_x[1]
        )
        turned[0:DEPTH, :] = jnp.where(live, carried, 0.0)
        turned[DEPTH : 2 * DEPTH, :] = jnp.where(live, put_in[1], 0.0)
        turned[2 * DEPTH : 2 * DEPTH + 8, :] = jnp.broadcast_to(
            jnp.where(live, both, 1.0), (8, LANES)
        )
        turned[2 * DEPTH + 8 :, :] = jnp.zeros((LANES - 2 * DEPTH - 8, LANES), jnp.float32)
        at = COEF + row * LANES
        pack[at : at + LANES, :] = jnp.transpose(turned[...])
        for k in range(3):
            at = TAIL_X + (row * 3 + k) * DEPTH
            pack[at : at + DEPTH, :] = jnp.where(live, frames_x[k + 2], frames_x[k])
            for b in range(2):
                entry = jnp.where(live, frames_bc[k + 2][b], frames_bc[k][b])
                at = TAIL_BC + ((row * 3 + k) * 2 + b) * 8
                pack[at : at + 4, :] = entry[:, :LANES]
                pack[at + 4 : at + 8, :] = entry[:, LANES:]

    def readout(row, octets, piece):
        def one_group(g, carry):
            c = [
                [rows_c[row, s, half, g] for half in range(2)] for s in range(STEPS)
            ]
            for octet in octets:
                held = [jnp.zeros((8, LANES), jnp.float32) for _ in range(STEPS)]
                for p in range(DEPTH):
                    left, right = piece(GROUPS * p + g, octet)
                    for s in range(STEPS):
                        dot = jnp.sum(
                            left * c[s][0] + right * c[s][1], axis=1, keepdims=True
                        )
                        held[s] = jnp.where(lane == p, dot, held[s])
                for s in range(STEPS):
                    at = pl.multiple_of(g * PER_GROUP + octet * 8, 8)
                    dots[s, pl.ds(at, 8), :] = held[s]
            return carry

        lax.fori_loop(0, GROUPS, one_group, 0)

    def finish(row):
        for s in range(STEPS):
            dot = jnp.transpose(dots[s])[0:DEPTH, :]
            gated = (decays[row, s] * dot + extras[row, s]) * gates[row, s]
            gates[row, s] = gated
            sums[row * STEPS + s : row * STEPS + s + 1, :] = jnp.sum(
                gated * gated, axis=0, keepdims=True
            )

    prepare(
        0,
        kept_slot,
        [tail_x[kept, k].astype(jnp.float32) for k in range(3)],
        [[tail_bc[kept, k, b].astype(jnp.float32) for b in range(2)] for k in range(3)],
    )
    sums[4:8, :] = jnp.zeros((4, LANES), jnp.float32)

    def kept_piece(at, octet):
        rows = state[kept, at, 8 * octet : 8 * octet + 8, :]
        return rows[:, :LANES], rows[:, LANES:]

    readout(0, range(PER_GROUP // 8), kept_piece)
    finish(0)

    def giver(to):
        from_low = lax.shift_right_logical(source[2 * to], 1)
        from_high = lax.shift_right_logical(source[2 * to + 1], 1)
        return jnp.where(from_low != to, from_low, from_high)

    for chunk in range(CHUNKS):
        all_pieces(0, chunk).wait_recv()

        def forward(i, carry, chunk=chunk):
            to = partner_of(me, i, devices)
            second[chunk][to] = spread[chunk][giver(to)]
            remote(1, chunk, to).start()
            return carry

        lax.fori_loop(1, devices, forward, 0)
        back[chunk][me] = spread[chunk][giver(me)]

    outs = [
        pltpu.make_async_copy(back_a, moved_a, out_sem.at[0]),
        pltpu.make_async_copy(back_b, moved_b, out_sem.at[1]),
        pltpu.make_async_copy(pack, pack_hbm, out_sem.at[2]),
    ]
    for chunk in range(CHUNKS):
        all_pieces(1, chunk).wait_recv()
        outs[chunk].start()
        if chunk == 0:

            def untail(k, carry):
                tails[64 + lax.rem(k, 32), :] = back_a[k, 2 * PART + 1, :]
                tails[k, :] = back_a[k, 2 * PART, :]
                return carry

            lax.fori_loop(0, devices, untail, 0)
            window_bc = [
                [
                    jnp.concatenate(
                        [
                            tails[48 + (2 * k + b) * 8 : 52 + (2 * k + b) * 8, :],
                            tails[52 + (2 * k + b) * 8 : 56 + (2 * k + b) * 8, :],
                        ],
                        axis=1,
                    )
                    for b in range(2)
                ]
                for k in range(3)
            ]
            prepare(
                1,
                moved_slot,
                [tails[DEPTH * k : DEPTH * (k + 1), :] for k in range(3)],
                window_bc,
            )

        def moved_piece(at, octet, chunk=chunk):
            within = 8 * octet - PART * chunk
            return (
                back[chunk][at, within : within + 8, :],
                back[chunk][at, PART + within : PART + within + 8, :],
            )

        readout(1, range(chunk * PART // 8, (chunk + 1) * PART // 8), moved_piece)
    finish(1)

    exchanges = [
        pltpu.make_async_remote_copy(
            src_ref=sums,
            dst_ref=sums_in.at[j - 1],
            send_sem=sum_send_sem.at[j - 1],
            recv_sem=sum_recv_sem.at[j - 1],
            device_id={"tp": lax.rem(column + j, TP)},
            device_id_type=MESH,
        )
        for j in range(1, TP)
    ]
    for exchange in exchanges:
        exchange.start()
    same_group = (
        lax.broadcasted_iota(jnp.int32, (LANES, LANES), 0) // PER_GROUP
        == lax.broadcasted_iota(jnp.int32, (LANES, LANES), 1) // PER_GROUP
    ).astype(jnp.float32)
    for exchange in exchanges:
        exchange.wait_recv()
    totals = jnp.dot(
        sums[...] + sums_in[0] + sums_in[1] + sums_in[2],
        same_group,
        preferred_element_type=jnp.float32,
        precision=lax.Precision.HIGHEST,
    )
    factor = lax.rsqrt(totals / (DEPTH * TP * PER_GROUP) + EPSILON)
    for row in range(2):
        live = active[jnp.where(row == 0, kept_slot, moved_slot)] == 1
        for s in range(STEPS):
            scale = factor[row * STEPS + s : row * STEPS + s + 1, :]
            at = Y_ROWS + (row * STEPS + s) * DEPTH
            pack[at : at + DEPTH, :] = jnp.where(
                live, gates[row, s] * scale * norm_gain[...], 0.0
            )
    outs[2].start()
    for exchange in exchanges:
        exchange.wait_send()
    for phase in range(2):
        for chunk in range(CHUNKS):
            all_pieces(phase, chunk).wait_send()
    for out in outs:
        out.wait()


QUARTERS = 4


def state_kernel(
    devices,
    source_hbm,
    state_hbm,
    moved_a_hbm,
    moved_b_hbm,
    pack_hbm,
    state_out,
    tail_x_out,
    tail_bc_out,
    y_out,
    source,
    kept_in,
    moved_a,
    moved_b,
    pack,
    result,
    tail_x,
    tail_bc,
    y,
    sem,
    part_sem,
):
    me = lax.axis_index("rows")
    size = devices // QUARTERS

    def piece_range(q):
        return pl.ds(q * size, size)

    source_load = pltpu.make_async_copy(source_hbm, source, sem.at[0])
    pack_load = pltpu.make_async_copy(pack_hbm, pack, sem.at[1])
    source_load.start()
    pack_load.start()
    moved_loads = [
        [
            pltpu.make_async_copy(
                hbm.at[piece_range(q)], vmem.at[piece_range(q)], part_sem.at[c, q]
            )
            for c, (hbm, vmem) in enumerate(((moved_a_hbm, moved_a), (moved_b_hbm, moved_b)))
        ]
        for q in range(QUARTERS)
    ]
    for pair in moved_loads:
        for load in pair:
            load.start()
    source_load.wait()
    low = source[2 * me]
    high = source[2 * me + 1]
    kept = 1 - given_of(low, high, me)
    kept_slot = jnp.where(low == 2 * me + kept, 0, 1)
    slots = (kept_slot, 1 - kept_slot)
    kept_loads = [
        pltpu.make_async_copy(
            state_hbm.at[kept, piece_range(q)], kept_in.at[piece_range(q)], part_sem.at[2, q]
        )
        for q in range(QUARTERS)
    ]
    for load in kept_loads:
        load.start()
    pack_load.wait()
    writes = []
    for row in (1, 0):
        base = COEF + row * LANES
        b = [
            pack[
                INPUT_B + (row * STEPS + s) * 8 : INPUT_B + (row * STEPS + s) * 8 + 8, :
            ]
            for s in range(STEPS)
        ]
        for q in range(QUARTERS):
            if row == 1:
                for load in moved_loads[q]:
                    load.wait()
            else:
                kept_loads[q].wait()
            for p in range(q * DEPTH // QUARTERS, (q + 1) * DEPTH // QUARTERS):
                for g in range(GROUPS):
                    k = GROUPS * p + g
                    for octet in range(PER_GROUP // 8):
                        head = base + g * PER_GROUP + octet * 8
                        u1 = pack[head : head + 8, p : p + 1]
                        u2 = pack[head : head + 8, DEPTH + p : DEPTH + p + 1]
                        decay = pack[head : head + 8, 2 * DEPTH : 2 * DEPTH + 1]
                        for half in range(2):
                            if row == 1:
                                chunk = octet * 8 // PART
                                at = half * PART + octet * 8 - chunk * PART
                                held = (moved_a, moved_b)[chunk][k, at : at + 8, :]
                            else:
                                held = kept_in[
                                    k,
                                    octet * 8 : octet * 8 + 8,
                                    half * LANES : (half + 1) * LANES,
                                ]
                            at = half * GROUPS + g
                            result[
                                row,
                                k,
                                octet * 8 : octet * 8 + 8,
                                half * LANES : (half + 1) * LANES,
                            ] = (
                                held * decay + u1 * b[0][at : at + 1, :] + u2 * b[1][at : at + 1, :]
                            )
            write = pltpu.make_async_copy(
                result.at[row, piece_range(q)],
                state_out.at[slots[row], piece_range(q)],
                part_sem.at[3 + row, q],
            )
            write.start()
            writes.append(write)
        slot = slots[row]
        for s in range(STEPS):
            at = Y_ROWS + (row * STEPS + s) * DEPTH
            y[s, slot] = pack[at : at + DEPTH, :].astype(jnp.bfloat16)
        for k in range(3):
            at = TAIL_X + (row * 3 + k) * DEPTH
            tail_x[slot, k] = pack[at : at + DEPTH, :].astype(jnp.bfloat16)
            for c in range(2):
                at = TAIL_BC + ((row * 3 + k) * 2 + c) * 8
                tail_bc[slot, k, c] = jnp.concatenate(
                    [pack[at : at + 4, :], pack[at + 4 : at + 8, :]], axis=1
                ).astype(jnp.bfloat16)
    for i, (vmem, hbm) in enumerate(((tail_x, tail_x_out), (tail_bc, tail_bc_out), (y, y_out))):
        write = pltpu.make_async_copy(vmem, hbm, sem.at[2 + i])
        write.start()
        writes.append(write)
    for write in writes:
        write.wait()


def on_device(
    state_in,
    tail_x,
    tail_bc,
    source,
    active,
    x_new,
    z_new,
    bc_new,
    dt_new,
    conv_wx,
    conv_bx,
    conv_wbc,
    conv_bbc,
    dt_bias,
    a_log,
    skip_d,
    norm_gain,
):
    devices = lax.axis_size("rows")
    slots, depth, head_count, width = state_in.shape
    pieces = state_in.reshape(slots, devices, PER_GROUP, width)
    operands = (
        source,
        active,
        pieces,
        tail_x,
        tail_bc,
        x_new,
        z_new,
        bc_new,
        dt_new,
        conv_wx,
        conv_bx,
        conv_wbc,
        conv_bbc,
        dt_bias.reshape(1, -1),
        a_log.reshape(1, -1),
        skip_d.reshape(1, -1),
        norm_gain,
    )
    long_buffer = pltpu.VMEM((devices, 2 * PART + TAIL_ROWS, LANES), jnp.float32)
    short_buffer = pltpu.VMEM((devices, 2 * PART, LANES), jnp.float32)
    hbm = pl.BlockSpec(memory_space=pltpu.HBM)
    moved_a, moved_b, pack = pl.pallas_call(
        functools.partial(relocate_kernel, devices),
        out_shape=(
            jax.ShapeDtypeStruct(long_buffer.shape, jnp.float32),
            jax.ShapeDtypeStruct(short_buffer.shape, jnp.float32),
            jax.ShapeDtypeStruct((PACK_ROWS, LANES), jnp.float32),
        ),
        in_specs=[hbm] * len(operands),
        out_specs=(hbm, hbm, hbm),
        scratch_shapes=[
            pltpu.SMEM(source.shape, jnp.int32),
            pltpu.SMEM(active.shape, jnp.int32),
        ]
        + [pltpu.VMEM(a.shape, a.dtype) for a in operands[2:]]
        + [pltpu.VMEM((96, LANES), jnp.float32)]
        + [long_buffer, short_buffer] * 4
        + [
            pltpu.VMEM((PACK_ROWS, LANES), jnp.float32),
            pltpu.VMEM((2, STEPS, 2, GROUPS, 8, LANES), jnp.float32),
            pltpu.VMEM((2, STEPS, DEPTH, LANES), jnp.float32),
            pltpu.VMEM((2, STEPS, DEPTH, LANES), jnp.float32),
            pltpu.VMEM((2, STEPS, DEPTH, LANES), jnp.float32),
            pltpu.VMEM((STEPS, LANES, LANES), jnp.float32),
            pltpu.VMEM((LANES, LANES), jnp.float32),
            pltpu.VMEM((8, LANES), jnp.float32),
            pltpu.VMEM((TP - 1, 8, LANES), jnp.float32),
            pltpu.SemaphoreType.DMA((len(operands),)),
            pltpu.SemaphoreType.DMA((2, CHUNKS)),
            pltpu.SemaphoreType.DMA((2, CHUNKS)),
            pltpu.SemaphoreType.DMA((TP - 1,)),
            pltpu.SemaphoreType.DMA((TP - 1,)),
            pltpu.SemaphoreType.DMA((3,)),
        ],
        compiler_params=pltpu.CompilerParams(
            collective_id=0, has_side_effects=True, vmem_limit_bytes=60 * 1024 * 1024
        ),
    )(*operands)
    state, window_x, window_bc, y = pl.pallas_call(
        functools.partial(state_kernel, devices),
        out_shape=(
            jax.ShapeDtypeStruct(pieces.shape, jnp.float32),
            jax.ShapeDtypeStruct(tail_x.shape, tail_x.dtype),
            jax.ShapeDtypeStruct(tail_bc.shape, tail_bc.dtype),
            jax.ShapeDtypeStruct(x_new.shape, jnp.bfloat16),
        ),
        in_specs=[hbm] * 5,
        out_specs=(hbm,) * 4,
        scratch_shapes=[
            pltpu.SMEM(source.shape, jnp.int32),
            pltpu.VMEM((devices, PER_GROUP, width), jnp.float32),
            long_buffer,
            short_buffer,
            pltpu.VMEM((PACK_ROWS, LANES), jnp.float32),
            pltpu.VMEM(pieces.shape, jnp.float32),
            pltpu.VMEM(tail_x.shape, tail_x.dtype),
            pltpu.VMEM(tail_bc.shape, tail_bc.dtype),
            pltpu.VMEM(x_new.shape, jnp.bfloat16),
            pltpu.SemaphoreType.DMA((5,)),
            pltpu.SemaphoreType.DMA((5, QUARTERS)),
        ],
        compiler_params=pltpu.CompilerParams(vmem_limit_bytes=60 * 1024 * 1024),
    )(source, pieces, moved_a, moved_b, pack)
    return state.reshape(state_in.shape), window_x, window_bc, y


def solution(mesh):
    return jax.shard_map(
        on_device,
        mesh=mesh,
        in_specs=(
            P("rows", "tp", None, None),
            P("rows", None, "tp", None),
            P("rows", None, None, None, None),
            P(),
            P("rows"),
            P(None, "rows", "tp", None),
            P(None, "rows", "tp", None),
            P(None, "rows", None, None, None),
            P(None, "rows", None),
            P(None, "tp", None),
            P("tp", None),
            P(),
            P(),
            P(),
            P(),
            P(),
            P("tp", None),
        ),
        out_specs=(
            P("rows", "tp", None, None),
            P("rows", None, "tp", None),
            P("rows", None, None, None, None),
            P(None, "rows", "tp", None),
        ),
        check_vma=False,
    )
```

```python
import functools
import jax
import jax.numpy as jnp
from jax import lax
from jax.experimental import pallas as pl
from jax.experimental.pallas import tpu as pltpu
from jax.sharding import PartitionSpec as P

STEPS = 2
EPSILON = 1e-05
MESH = pl.DeviceIdType.MESH
CHUNKS = 2
TAIL_ROWS = 2
LANES = 128
DEPTH = 16
GROUPS = 4
PER_GROUP = 32
PART = PER_GROUP // CHUNKS
TP = 4

Y_ROWS = 0
TAIL_X = 64
TAIL_BC = 160
PACK_ROWS = 256


def silu(v):
    return v / (1.0 + jnp.exp(-v))


def partner_of(me, i, devices):
    return lax.rem(me + i, devices)


def given_of(low, high, me):
    return jnp.where((low != 2 * me) & (high != 2 * me), 0, 1)


def relocate_kernel(
    devices,
    source_hbm,
    active_hbm,
    state_hbm,
    tail_x_hbm,
    tail_bc_hbm,
    x_new_hbm,
    z_new_hbm,
    bc_new_hbm,
    dt_new_hbm,
    conv_wx_hbm,
    conv_bx_hbm,
    conv_wbc_hbm,
    conv_bbc_hbm,
    dt_bias_hbm,
    a_log_hbm,
    skip_d_hbm,
    final_hbm,
    pack_hbm,
    sums_hbm,
    source,
    active,
    state,
    tail_x,
    tail_bc,
    x_new,
    z_new,
    bc_new,
    dt_new,
    conv_wx,
    conv_bx,
    conv_wbc,
    conv_bbc,
    dt_bias,
    a_log,
    skip_d,
    tails,
    first_a,
    first_b,
    spread_a,
    spread_b,
    second_a,
    second_b,
    back_a,
    back_b,
    pack,
    final,
    rows_b,
    rows_c,
    factors,
    decays,
    extras,
    gates,
    dots,
    turned,
    sums,
    load_sem,
    send_sem,
    recv_sem,
    sum_send_sem,
    sum_recv_sem,
    out_sem,
):
    me = lax.axis_index("rows")
    column = lax.axis_index("tp")
    first, spread, second, back = (
        (first_a, first_b),
        (spread_a, spread_b),
        (second_a, second_b),
        (back_a, back_b),
    )
    loads = [
        pltpu.make_async_copy(src, dst, load_sem.at[i])
        for i, (src, dst) in enumerate(
            (
                (source_hbm, source),
                (tail_x_hbm, tail_x),
                (tail_bc_hbm, tail_bc),
                (state_hbm, state),
                (active_hbm, active),
                (x_new_hbm, x_new),
                (z_new_hbm, z_new),
                (bc_new_hbm, bc_new),
                (dt_new_hbm, dt_new),
                (conv_wx_hbm, conv_wx),
                (conv_bx_hbm, conv_bx),
                (conv_wbc_hbm, conv_wbc),
                (conv_bbc_hbm, conv_bbc),
                (dt_bias_hbm, dt_bias),
                (a_log_hbm, a_log),
                (skip_d_hbm, skip_d),
            )
        )
    ]
    for load in loads:
        load.start()
    barrier = pltpu.get_barrier_semaphore()

    def greet(i, carry):
        pl.semaphore_signal(
            barrier,
            inc=1,
            device_id={"rows": partner_of(me, i, devices)},
            device_id_type=MESH,
        )
        return carry

    lax.fori_loop(1, devices, greet, 0)
    for j in range(1, TP):
        pl.semaphore_signal(
            barrier,
            inc=1,
            device_id={"tp": lax.rem(column + j, TP)},
            device_id_type=MESH,
        )

    loads[0].wait()
    low = source[2 * me]
    high = source[2 * me + 1]
    given = given_of(low, high, me)
    kept = 1 - given
    kept_slot = jnp.where(low == 2 * me + kept, 0, 1)
    moved_slot = 1 - kept_slot

    loads[1].wait()
    loads[2].wait()
    for k in range(3):
        tails[DEPTH * k : DEPTH * (k + 1), :] = tail_x[given, k].astype(jnp.float32)
        for b in range(2):
            entry = tail_bc[given, k, b].astype(jnp.float32)
            at = 48 + (2 * k + b) * 8
            tails[at : at + 4, :] = entry[:, :LANES]
            tails[at + 4 : at + 8, :] = entry[:, LANES:]

    def remote(phase, chunk, to):
        source_ref, target_ref = ((first, spread), (second, back))[phase]
        return pltpu.make_async_remote_copy(
            src_ref=source_ref[chunk].at[to],
            dst_ref=target_ref[chunk].at[me],
            send_sem=send_sem.at[phase, chunk],
            recv_sem=recv_sem.at[phase, chunk],
            device_id={"rows": to},
            device_id_type=MESH,
        )

    def all_pieces(phase, chunk):
        source_ref, target_ref = ((first, spread), (second, back))[phase]
        return pltpu.make_async_remote_copy(
            src_ref=source_ref[chunk].at[pl.ds(0, devices - 1)],
            dst_ref=target_ref[chunk].at[pl.ds(0, devices - 1)],
            send_sem=send_sem.at[phase, chunk],
            recv_sem=recv_sem.at[phase, chunk],
            device_id={"rows": partner_of(me, 1, devices)},
            device_id_type=MESH,
        )

    def fill(chunk, piece, into, at):
        rows = state[given, piece, chunk * PART : (chunk + 1) * PART, :]
        into[at, 0:PART, :] = rows[:, :LANES]
        into[at, PART : 2 * PART, :] = rows[:, LANES:]
        if chunk == 0:
            into[at, 2 * PART, :] = tails[piece, :]
            into[at, 2 * PART + 1, :] = tails[64 + lax.rem(piece, 32), :]

    loads[3].wait()
    pl.semaphore_wait(barrier, devices - 1 + TP - 1)
    for chunk in range(CHUNKS):

        def begin(i, carry, chunk=chunk):
            to = partner_of(me, i, devices)
            fill(chunk, to, first[chunk], to)
            remote(0, chunk, to).start()
            return carry

        lax.fori_loop(1, devices, begin, 0)
        fill(chunk, me, spread[chunk], me)

    for load in loads[4:]:
        load.wait()
    group_of_lane = lax.broadcasted_iota(jnp.int32, (GROUPS, LANES), 1) // PER_GROUP
    own_group = group_of_lane == lax.broadcasted_iota(jnp.int32, (GROUPS, LANES), 0)
    lane = lax.broadcasted_iota(jnp.int32, (8, LANES), 1)

    def by_head(values):
        return jnp.sum(jnp.where(own_group, values, 0.0), axis=0, keepdims=True)

    def prepare(row, slot, window_x, window_bc):
        live = active[slot] == 1
        new_x = [x_new[s, slot].astype(jnp.float32) for s in range(STEPS)]
        new_bc = [
            [bc_new[s, slot, b].astype(jnp.float32) for b in range(2)] for s in range(STEPS)
        ]
        frames_x = window_x + new_x
        frames_bc = window_bc + new_bc
        conv_x = []
        conv_b = []
        conv_c = []
        sizes = []
        decay = []
        rate = jnp.exp(a_log[...])
        for s in range(STEPS):
            total = frames_x[s] * conv_wx[0]
            for k in range(1, 4):
                total = total + frames_x[s + k] * conv_wx[k]
            conv_x.append(silu(total + conv_bx[...]))
            pair = []
            for b in range(2):
                total = frames_bc[s][b] * conv_wbc[0, b]
                for k in range(1, 4):
                    total = total + frames_bc[s + k][b] * conv_wbc[k, b]
                pair.append(silu(total + conv_bbc[b]))
            conv_b.append(pair[0])
            conv_c.append(pair[1])
            raw = jnp.where(slot == 0, dt_new[s, 0:1, :], dt_new[s, 1:2, :]) + dt_bias[...]
            size = jnp.maximum(raw, 0.0) + jnp.log1p(jnp.exp(-jnp.abs(raw)))
            sizes.append(size)
            decay.append(jnp.exp(-size * rate))
            for half in range(2):
                for g in range(GROUPS):
                    at = slice(half * LANES, (half + 1) * LANES)
                    rows_b[row, s, half, g] = jnp.broadcast_to(pair[0][g : g + 1, at], (8, LANES))
                    rows_c[row, s, half, g] = jnp.broadcast_to(pair[1][g : g + 1, at], (8, LANES))
            gates[row, s] = silu(z_new[s, slot].astype(jnp.float32))

        def overlap(i, j):
            return by_head(jnp.sum(conv_b[i] * conv_c[j], axis=1, keepdims=True))

        skip = skip_d[...]
        put_in = [sizes[s] * conv_x[s] for s in range(STEPS)]
        carried = put_in[0] * decay[1]
        both = decay[0] * decay[1]
        decays[row, 0] = jnp.broadcast_to(decay[0], (DEPTH, LANES))
        decays[row, 1] = jnp.broadcast_to(both, (DEPTH, LANES))
        extras[row, 0] = put_in[0] * overlap(0, 0) + skip * conv_x[0]
        extras[row, 1] = (
            carried * overlap(0, 1) + put_in[1] * overlap(1, 1) + skip * conv_x[1]
        )
        turned[0:DEPTH, :] = jnp.where(live, carried, 0.0)
        turned[DEPTH : 2 * DEPTH, :] = jnp.where(live, put_in[1], 0.0)
        turned[2 * DEPTH : 2 * DEPTH + 8, :] = jnp.broadcast_to(
            jnp.where(live, both, 1.0), (8, LANES)
        )
        turned[2 * DEPTH + 8 :, :] = jnp.zeros((LANES - 2 * DEPTH - 8, LANES), jnp.float32)
        factors[row] = jnp.transpose(turned[...])
        for k in range(3):
            at = TAIL_X + (row * 3 + k) * DEPTH
            pack[at : at + DEPTH, :] = jnp.where(live, frames_x[k + 2], frames_x[k])
            for b in range(2):
                entry = jnp.where(live, frames_bc[k + 2][b], frames_bc[k][b])
                at = TAIL_BC + ((row * 3 + k) * 2 + b) * 8
                pack[at : at + 4, :] = entry[:, :LANES]
                pack[at + 4 : at + 8, :] = entry[:, LANES:]

    def readout(row, octets, piece):
        def one_group(g, carry):
            c = [
                [rows_c[row, s, half, g] for half in range(2)] for s in range(STEPS)
            ]
            for octet in octets:
                held = [jnp.zeros((8, LANES), jnp.float32) for _ in range(STEPS)]
                for p in range(DEPTH):
                    left, right = piece(GROUPS * p + g, octet)
                    for s in range(STEPS):
                        dot = jnp.sum(
                            left * c[s][0] + right * c[s][1], axis=1, keepdims=True
                        )
                        held[s] = jnp.where(lane == p, dot, held[s])
                for s in range(STEPS):
                    at = pl.multiple_of(g * PER_GROUP + octet * 8, 8)
                    dots[s, pl.ds(at, 8), :] = held[s]
            return carry

        lax.fori_loop(0, GROUPS, one_group, 0)

    def update(row, octets, piece):
        def one_group(g, carry):
            b = [[rows_b[row, s, half, g] for half in range(2)] for s in range(STEPS)]
            for octet in octets:
                heads = pl.ds(pl.multiple_of(g * PER_GROUP + octet * 8, 8), 8)

                def spread_out(at):
                    return jnp.broadcast_to(factors[row, heads, at : at + 1], (8, LANES))

                decay = spread_out(2 * DEPTH)
                for p in range(DEPTH):
                    u1 = spread_out(p)
                    u2 = spread_out(DEPTH + p)
                    k = GROUPS * p + g
                    for half, held in enumerate(piece(k, octet)):
                        final[
                            row,
                            k,
                            8 * octet : 8 * octet + 8,
                            half * LANES : (half + 1) * LANES,
                        ] = held * decay + u1 * b[0][half] + u2 * b[1][half]
            return carry

        lax.fori_loop(0, GROUPS, one_group, 0)

    def finish(row):
        for s in range(STEPS):
            dot = jnp.transpose(dots[s])[0:DEPTH, :]
            gated = (decays[row, s] * dot + extras[row, s]) * gates[row, s]
            at = Y_ROWS + (row * STEPS + s) * DEPTH
            pack[at : at + DEPTH, :] = gated
            sums[row * STEPS + s : row * STEPS + s + 1, :] = jnp.sum(
                gated * gated, axis=0, keepdims=True
            )

    prepare(
        0,
        kept_slot,
        [tail_x[kept, k].astype(jnp.float32) for k in range(3)],
        [[tail_bc[kept, k, b].astype(jnp.float32) for b in range(2)] for k in range(3)],
    )
    sums[4:8, :] = jnp.zeros((4, LANES), jnp.float32)

    def kept_piece(at, octet):
        rows = state[kept, at, 8 * octet : 8 * octet + 8, :]
        return rows[:, :LANES], rows[:, LANES:]

    readout(0, range(PER_GROUP // 8), kept_piece)
    finish(0)
    update(0, range(PER_GROUP // 8), kept_piece)
    outs = [
        pltpu.make_async_copy(final.at[0], final_hbm.at[0], out_sem.at[0]),
        pltpu.make_async_copy(pack, pack_hbm, out_sem.at[1]),
    ] + [
        pltpu.make_async_copy(
            final.at[1, :, pl.ds(chunk * PART, PART), :],
            final_hbm.at[1, :, pl.ds(chunk * PART, PART), :],
            out_sem.at[2 + chunk],
        )
        for chunk in range(CHUNKS)
    ] + [pltpu.make_async_copy(sums, sums_hbm.at[0], out_sem.at[2 + CHUNKS])]
    outs[0].start()

    def giver(to):
        from_low = lax.shift_right_logical(source[2 * to], 1)
        from_high = lax.shift_right_logical(source[2 * to + 1], 1)
        return jnp.where(from_low != to, from_low, from_high)

    for chunk in range(CHUNKS):
        all_pieces(0, chunk).wait_recv()

        def forward(i, carry, chunk=chunk):
            to = partner_of(me, i, devices)
            second[chunk][to] = spread[chunk][giver(to)]
            remote(1, chunk, to).start()
            return carry

        lax.fori_loop(1, devices, forward, 0)
        back[chunk][me] = spread[chunk][giver(me)]

    for chunk in range(CHUNKS):
        all_pieces(1, chunk).wait_recv()
        if chunk == 0:

            def untail(k, carry):
                tails[64 + lax.rem(k, 32), :] = back_a[k, 2 * PART + 1, :]
                tails[k, :] = back_a[k, 2 * PART, :]
                return carry

            lax.fori_loop(0, devices, untail, 0)
            window_bc = [
                [
                    jnp.concatenate(
                        [
                            tails[48 + (2 * k + b) * 8 : 52 + (2 * k + b) * 8, :],
                            tails[52 + (2 * k + b) * 8 : 56 + (2 * k + b) * 8, :],
                        ],
                        axis=1,
                    )
                    for b in range(2)
                ]
                for k in range(3)
            ]
            prepare(
                1,
                moved_slot,
                [tails[DEPTH * k : DEPTH * (k + 1), :] for k in range(3)],
                window_bc,
            )

        def moved_piece(at, octet, chunk=chunk):
            within = 8 * octet - PART * chunk
            return (
                back[chunk][at, within : within + 8, :],
                back[chunk][at, PART + within : PART + within + 8, :],
            )

        octets = range(chunk * PART // 8, (chunk + 1) * PART // 8)
        readout(1, octets, moved_piece)
        if chunk < CHUNKS - 1:
            update(1, octets, moved_piece)
            outs[2 + chunk].start()
    finish(1)

    exchanges = [
        pltpu.make_async_remote_copy(
            src_ref=sums,
            dst_ref=sums_hbm.at[j],
            send_sem=sum_send_sem.at[j - 1],
            recv_sem=sum_recv_sem.at[j - 1],
            device_id={"tp": lax.rem(column + j, TP)},
            device_id_type=MESH,
        )
        for j in range(1, TP)
    ]
    for exchange in exchanges:
        exchange.start()
    for at in (1, 2 + CHUNKS):
        outs[at].start()
    update(1, octets, moved_piece)
    outs[1 + CHUNKS].start()
    for exchange in exchanges:
        exchange.wait_recv()
    for exchange in exchanges:
        exchange.wait_send()
    for phase in range(2):
        for chunk in range(CHUNKS):
            all_pieces(phase, chunk).wait_send()
    for out in outs:
        out.wait()


PARTS = 2


def place_kernel(
    devices,
    source_hbm,
    active_hbm,
    norm_gain_hbm,
    sums_hbm,
    final_hbm,
    pack_hbm,
    state_out,
    tail_x_out,
    tail_bc_out,
    y_out,
    source,
    active,
    norm_gain,
    sums,
    held,
    pack,
    tail_x,
    tail_bc,
    y,
    sem,
    part_sem,
):
    me = lax.axis_index("rows")
    size = devices // PARTS
    source_load = pltpu.make_async_copy(source_hbm, source, sem.at[0])
    small_loads = [
        pltpu.make_async_copy(hbm, vmem, sem.at[1 + i])
        for i, (hbm, vmem) in enumerate(
            (
                (sums_hbm, sums),
                (pack_hbm, pack),
                (active_hbm, active),
                (norm_gain_hbm, norm_gain),
            )
        )
    ]
    source_load.start()
    for load in small_loads:
        load.start()
    parts = [(row, q) for row in range(2) for q in range(PARTS)]
    loads = [
        pltpu.make_async_copy(
            final_hbm.at[row, pl.ds(q * size, size)],
            held.at[row, pl.ds(q * size, size)],
            part_sem.at[row, q],
        )
        for row, q in parts
    ]
    for load in loads:
        load.start()
    source_load.wait()
    low = source[2 * me]
    high = source[2 * me + 1]
    kept = 1 - given_of(low, high, me)
    kept_slot = jnp.where(low == 2 * me + kept, 0, 1)
    slots = (kept_slot, 1 - kept_slot)
    writes = []
    for load, (row, q) in zip(loads, parts):
        load.wait()
        write = pltpu.make_async_copy(
            held.at[row, pl.ds(q * size, size)],
            state_out.at[slots[row], pl.ds(q * size, size)],
            part_sem.at[2 + row, q],
        )
        write.start()
        writes.append(write)
    for load in small_loads:
        load.wait()
    same_group = (
        lax.broadcasted_iota(jnp.int32, (LANES, LANES), 0) // PER_GROUP
        == lax.broadcasted_iota(jnp.int32, (LANES, LANES), 1) // PER_GROUP
    ).astype(jnp.float32)
    totals = jnp.dot(
        sums[0] + sums[1] + sums[2] + sums[3],
        same_group,
        preferred_element_type=jnp.float32,
        precision=lax.Precision.HIGHEST,
    )
    factor = lax.rsqrt(totals / (DEPTH * TP * PER_GROUP) + EPSILON)
    for row, slot in enumerate(slots):
        live = active[slot] == 1
        for s in range(STEPS):
            scale = factor[row * STEPS + s : row * STEPS + s + 1, :]
            at = Y_ROWS + (row * STEPS + s) * DEPTH
            scaled = pack[at : at + DEPTH, :] * scale * norm_gain[...]
            y[s, slot] = jnp.where(live, scaled, 0.0).astype(jnp.bfloat16)
        for k in range(3):
            at = TAIL_X + (row * 3 + k) * DEPTH
            tail_x[slot, k] = pack[at : at + DEPTH, :].astype(jnp.bfloat16)
            for c in range(2):
                at = TAIL_BC + ((row * 3 + k) * 2 + c) * 8
                tail_bc[slot, k, c] = jnp.concatenate(
                    [pack[at : at + 4, :], pack[at + 4 : at + 8, :]], axis=1
                ).astype(jnp.bfloat16)
    for i, (vmem, hbm) in enumerate(((tail_x, tail_x_out), (tail_bc, tail_bc_out), (y, y_out))):
        write = pltpu.make_async_copy(vmem, hbm, sem.at[5 + i])
        write.start()
        writes.append(write)
    for write in writes:
        write.wait()


def on_device(
    state_in,
    tail_x,
    tail_bc,
    source,
    active,
    x_new,
    z_new,
    bc_new,
    dt_new,
    conv_wx,
    conv_bx,
    conv_wbc,
    conv_bbc,
    dt_bias,
    a_log,
    skip_d,
    norm_gain,
):
    devices = lax.axis_size("rows")
    slots, depth, head_count, width = state_in.shape
    pieces = state_in.reshape(slots, devices, PER_GROUP, width)
    operands = (
        source,
        active,
        pieces,
        tail_x,
        tail_bc,
        x_new,
        z_new,
        bc_new,
        dt_new,
        conv_wx,
        conv_bx,
        conv_wbc,
        conv_bbc,
        dt_bias.reshape(1, -1),
        a_log.reshape(1, -1),
        skip_d.reshape(1, -1),
    )
    long_buffer = pltpu.VMEM((devices, 2 * PART + TAIL_ROWS, LANES), jnp.float32)
    short_buffer = pltpu.VMEM((devices, 2 * PART, LANES), jnp.float32)
    hbm = pl.BlockSpec(memory_space=pltpu.HBM)
    final, pack, sums = pl.pallas_call(
        functools.partial(relocate_kernel, devices),
        out_shape=(
            jax.ShapeDtypeStruct(pieces.shape, jnp.float32),
            jax.ShapeDtypeStruct((PACK_ROWS, LANES), jnp.float32),
            jax.ShapeDtypeStruct((TP, 8, LANES), jnp.float32),
        ),
        in_specs=[hbm] * len(operands),
        out_specs=(hbm, hbm, hbm),
        scratch_shapes=[
            pltpu.SMEM(source.shape, jnp.int32),
            pltpu.SMEM(active.shape, jnp.int32),
        ]
        + [pltpu.VMEM(a.shape, a.dtype) for a in operands[2:]]
        + [pltpu.VMEM((96, LANES), jnp.float32)]
        + [long_buffer, short_buffer] * 4
        + [
            pltpu.VMEM((PACK_ROWS, LANES), jnp.float32),
            pltpu.VMEM(pieces.shape, jnp.float32),
            pltpu.VMEM((2, STEPS, 2, GROUPS, 8, LANES), jnp.float32),
            pltpu.VMEM((2, STEPS, 2, GROUPS, 8, LANES), jnp.float32),
            pltpu.VMEM((2, LANES, LANES), jnp.float32),
            pltpu.VMEM((2, STEPS, DEPTH, LANES), jnp.float32),
            pltpu.VMEM((2, STEPS, DEPTH, LANES), jnp.float32),
            pltpu.VMEM((2, STEPS, DEPTH, LANES), jnp.float32),
            pltpu.VMEM((STEPS, LANES, LANES), jnp.float32),
            pltpu.VMEM((LANES, LANES), jnp.float32),
            pltpu.VMEM((8, LANES), jnp.float32),
            pltpu.SemaphoreType.DMA((len(operands),)),
            pltpu.SemaphoreType.DMA((2, CHUNKS)),
            pltpu.SemaphoreType.DMA((2, CHUNKS)),
            pltpu.SemaphoreType.DMA((TP - 1,)),
            pltpu.SemaphoreType.DMA((TP - 1,)),
            pltpu.SemaphoreType.DMA((3 + CHUNKS,)),
        ],
        compiler_params=pltpu.CompilerParams(
            collective_id=0, has_side_effects=True, vmem_limit_bytes=60 * 1024 * 1024
        ),
    )(*operands)
    state, window_x, window_bc, y = pl.pallas_call(
        functools.partial(place_kernel, devices),
        out_shape=(
            jax.ShapeDtypeStruct(pieces.shape, jnp.float32),
            jax.ShapeDtypeStruct(tail_x.shape, tail_x.dtype),
            jax.ShapeDtypeStruct(tail_bc.shape, tail_bc.dtype),
            jax.ShapeDtypeStruct(x_new.shape, jnp.bfloat16),
        ),
        in_specs=[hbm] * 6,
        out_specs=(hbm,) * 4,
        scratch_shapes=[
            pltpu.SMEM(source.shape, jnp.int32),
            pltpu.SMEM(active.shape, jnp.int32),
            pltpu.VMEM(norm_gain.shape, jnp.float32),
            pltpu.VMEM((TP, 8, LANES), jnp.float32),
            pltpu.VMEM(pieces.shape, jnp.float32),
            pltpu.VMEM((PACK_ROWS, LANES), jnp.float32),
            pltpu.VMEM(tail_x.shape, tail_x.dtype),
            pltpu.VMEM(tail_bc.shape, tail_bc.dtype),
            pltpu.VMEM(x_new.shape, jnp.bfloat16),
            pltpu.SemaphoreType.DMA((8,)),
            pltpu.SemaphoreType.DMA((4, PARTS)),
        ],
        compiler_params=pltpu.CompilerParams(vmem_limit_bytes=60 * 1024 * 1024),
    )(source, active, norm_gain, sums, final, pack)
    return state.reshape(state_in.shape), window_x, window_bc, y


def solution(mesh):
    return jax.shard_map(
        on_device,
        mesh=mesh,
        in_specs=(
            P("rows", "tp", None, None),
            P("rows", None, "tp", None),
            P("rows", None, None, None, None),
            P(),
            P("rows"),
            P(None, "rows", "tp", None),
            P(None, "rows", "tp", None),
            P(None, "rows", None, None, None),
            P(None, "rows", None),
            P(None, "tp", None),
            P("tp", None),
            P(),
            P(),
            P(),
            P(),
            P(),
            P("tp", None),
        ),
        out_specs=(
            P("rows", "tp", None, None),
            P("rows", None, "tp", None),
            P("rows", None, None, None, None),
            P(None, "rows", "tp", None),
        ),
        check_vma=False,
    )
```

```python
import functools
import jax
import jax.numpy as jnp
from jax import lax
from jax.experimental import pallas as pl
from jax.experimental.pallas import tpu as pltpu
from jax.sharding import PartitionSpec as P

STEPS = 2
EPSILON = 1e-05
MESH = pl.DeviceIdType.MESH
CHUNKS = 2
TAIL_X_ROWS = 48
LANES = 128
DEPTH = 16
GROUPS = 4
PER_GROUP = 32
PART = PER_GROUP // CHUNKS
TP = 4

Y_ROWS = 0
TAIL_X = 64
TAIL_BC = 160
PACK_ROWS = 256


def silu(v):
    return v / (1.0 + jnp.exp(-v))


def partner_of(me, i, devices):
    return lax.rem(me + i, devices)


def given_of(low, high, me):
    return jnp.where((low != 2 * me) & (high != 2 * me), 0, 1)


def relocate_kernel(
    devices,
    source_hbm,
    active_hbm,
    state_hbm,
    tail_x_hbm,
    tail_bc_hbm,
    x_new_hbm,
    z_new_hbm,
    bc_new_hbm,
    dt_new_hbm,
    conv_wx_hbm,
    conv_bx_hbm,
    conv_wbc_hbm,
    conv_bbc_hbm,
    dt_bias_hbm,
    a_log_hbm,
    skip_d_hbm,
    final_hbm,
    pack_hbm,
    sums_hbm,
    source,
    active,
    state,
    tail_x,
    tail_bc,
    x_new,
    z_new,
    bc_new,
    dt_new,
    conv_wx,
    conv_bx,
    conv_wbc,
    conv_bbc,
    dt_bias,
    a_log,
    skip_d,
    tails,
    quarter,
    quarters,
    first_a,
    first_b,
    spread_a,
    spread_b,
    second_a,
    second_b,
    back_a,
    back_b,
    pack,
    final,
    rows_b,
    rows_c,
    factors,
    decays,
    extras,
    gates,
    dots,
    turned,
    sums,
    load_sem,
    send_sem,
    recv_sem,
    sum_send_sem,
    sum_recv_sem,
    share_send_sem,
    share_recv_sem,
    out_sem,
):
    me = lax.axis_index("rows")
    column = lax.axis_index("tp")
    first, spread, second, back = (
        (first_a, first_b),
        (spread_a, spread_b),
        (second_a, second_b),
        (back_a, back_b),
    )
    loads = [
        pltpu.make_async_copy(src, dst, load_sem.at[i])
        for i, (src, dst) in enumerate(
            (
                (source_hbm, source),
                (tail_x_hbm, tail_x),
                (tail_bc_hbm, tail_bc),
                (state_hbm, state),
                (active_hbm, active),
                (x_new_hbm, x_new),
                (z_new_hbm, z_new),
                (bc_new_hbm, bc_new),
                (dt_new_hbm, dt_new),
                (conv_wx_hbm, conv_wx),
                (conv_bx_hbm, conv_bx),
                (conv_wbc_hbm, conv_wbc),
                (conv_bbc_hbm, conv_bbc),
                (dt_bias_hbm, dt_bias),
                (a_log_hbm, a_log),
                (skip_d_hbm, skip_d),
            )
        )
    ]
    for load in loads:
        load.start()
    barrier = pltpu.get_barrier_semaphore()

    def greet(i, carry):
        pl.semaphore_signal(
            barrier,
            inc=1,
            device_id={"rows": partner_of(me, i, devices)},
            device_id_type=MESH,
        )
        return carry

    lax.fori_loop(1, devices, greet, 0)
    for j in range(1, TP):
        pl.semaphore_signal(
            barrier,
            inc=1,
            device_id={"tp": lax.rem(column + j, TP)},
            device_id_type=MESH,
        )

    loads[0].wait()
    low = source[2 * me]
    high = source[2 * me + 1]
    given = given_of(low, high, me)
    kept = 1 - given
    kept_slot = jnp.where(low == 2 * me + kept, 0, 1)
    moved_slot = 1 - kept_slot

    loads[1].wait()
    loads[2].wait()
    for k in range(3):
        tails[DEPTH * k : DEPTH * (k + 1), :] = tail_x[given, k].astype(jnp.float32)
        for b in range(2):
            entry = tail_bc[given, k, b].astype(jnp.float32)
            at = 48 + (2 * k + b) * 8
            tails[at : at + 4, :] = entry[:, :LANES]
            tails[at + 4 : at + 8, :] = entry[:, LANES:]

    def remote(phase, chunk, to):
        source_ref, target_ref = ((first, spread), (second, back))[phase]
        return pltpu.make_async_remote_copy(
            src_ref=source_ref[chunk].at[to],
            dst_ref=target_ref[chunk].at[me],
            send_sem=send_sem.at[phase, chunk],
            recv_sem=recv_sem.at[phase, chunk],
            device_id={"rows": to},
            device_id_type=MESH,
        )

    def all_pieces(phase, chunk):
        source_ref, target_ref = ((first, spread), (second, back))[phase]
        return pltpu.make_async_remote_copy(
            src_ref=source_ref[chunk].at[pl.ds(0, devices - 1)],
            dst_ref=target_ref[chunk].at[pl.ds(0, devices - 1)],
            send_sem=send_sem.at[phase, chunk],
            recv_sem=recv_sem.at[phase, chunk],
            device_id={"rows": partner_of(me, 1, devices)},
            device_id_type=MESH,
        )

    share = TAIL_X_ROWS // TP

    def fill(chunk, piece, into, at):
        rows = state[given, piece, chunk * PART : (chunk + 1) * PART, :]
        into[at, 0:PART, :] = rows[:, :LANES]
        into[at, PART : 2 * PART, :] = rows[:, LANES:]
        if chunk == 0:
            entry = TAIL_X_ROWS + share * column + lax.rem(piece, share)
            into[at, 2 * PART, :] = tails[jnp.where(piece < TAIL_X_ROWS, piece, entry), :]

    loads[3].wait()
    pl.semaphore_wait(barrier, devices - 1 + TP - 1)
    for chunk in range(CHUNKS):

        def begin(i, carry, chunk=chunk):
            to = partner_of(me, i, devices)
            fill(chunk, to, first[chunk], to)
            remote(0, chunk, to).start()
            return carry

        lax.fori_loop(1, devices, begin, 0)
        fill(chunk, me, spread[chunk], me)

    for load in loads[4:]:
        load.wait()
    group_of_lane = lax.broadcasted_iota(jnp.int32, (GROUPS, LANES), 1) // PER_GROUP
    own_group = group_of_lane == lax.broadcasted_iota(jnp.int32, (GROUPS, LANES), 0)
    lane = lax.broadcasted_iota(jnp.int32, (8, LANES), 1)

    def by_head(values):
        return jnp.sum(jnp.where(own_group, values, 0.0), axis=0, keepdims=True)

    def prepare(row, slot, window_x, window_bc):
        live = active[slot] == 1
        new_x = [x_new[s, slot].astype(jnp.float32) for s in range(STEPS)]
        new_bc = [
            [bc_new[s, slot, b].astype(jnp.float32) for b in range(2)] for s in range(STEPS)
        ]
        frames_x = window_x + new_x
        frames_bc = window_bc + new_bc
        conv_x = []
        conv_b = []
        conv_c = []
        sizes = []
        decay = []
        rate = jnp.exp(a_log[...])
        for s in range(STEPS):
            total = frames_x[s] * conv_wx[0]
            for k in range(1, 4):
                total = total + frames_x[s + k] * conv_wx[k]
            conv_x.append(silu(total + conv_bx[...]))
            pair = []
            for b in range(2):
                total = frames_bc[s][b] * conv_wbc[0, b]
                for k in range(1, 4):
                    total = total + frames_bc[s + k][b] * conv_wbc[k, b]
                pair.append(silu(total + conv_bbc[b]))
            conv_b.append(pair[0])
            conv_c.append(pair[1])
            raw = jnp.where(slot == 0, dt_new[s, 0:1, :], dt_new[s, 1:2, :]) + dt_bias[...]
            size = jnp.maximum(raw, 0.0) + jnp.log1p(jnp.exp(-jnp.abs(raw)))
            sizes.append(size)
            decay.append(jnp.exp(-size * rate))
            for half in range(2):
                for g in range(GROUPS):
                    at = slice(half * LANES, (half + 1) * LANES)
                    rows_b[row, s, half, g] = jnp.broadcast_to(pair[0][g : g + 1, at], (8, LANES))
                    rows_c[row, s, half, g] = jnp.broadcast_to(pair[1][g : g + 1, at], (8, LANES))
            gates[row, s] = silu(z_new[s, slot].astype(jnp.float32))

        def overlap(i, j):
            return by_head(jnp.sum(conv_b[i] * conv_c[j], axis=1, keepdims=True))

        skip = skip_d[...]
        put_in = [sizes[s] * conv_x[s] for s in range(STEPS)]
        carried = put_in[0] * decay[1]
        both = decay[0] * decay[1]
        decays[row, 0] = jnp.broadcast_to(decay[0], (DEPTH, LANES))
        decays[row, 1] = jnp.broadcast_to(both, (DEPTH, LANES))
        extras[row, 0] = put_in[0] * overlap(0, 0) + skip * conv_x[0]
        extras[row, 1] = (
            carried * overlap(0, 1) + put_in[1] * overlap(1, 1) + skip * conv_x[1]
        )
        turned[0:DEPTH, :] = jnp.where(live, carried, 0.0)
        turned[DEPTH : 2 * DEPTH, :] = jnp.where(live, put_in[1], 0.0)
        turned[2 * DEPTH : 2 * DEPTH + 8, :] = jnp.broadcast_to(
            jnp.where(live, both, 1.0), (8, LANES)
        )
        turned[2 * DEPTH + 8 :, :] = jnp.zeros((LANES - 2 * DEPTH - 8, LANES), jnp.float32)
        factors[row] = jnp.transpose(turned[...])
        for k in range(3):
            at = TAIL_X + (row * 3 + k) * DEPTH
            pack[at : at + DEPTH, :] = jnp.where(live, frames_x[k + 2], frames_x[k])
            for b in range(2):
                entry = jnp.where(live, frames_bc[k + 2][b], frames_bc[k][b])
                at = TAIL_BC + ((row * 3 + k) * 2 + b) * 8
                pack[at : at + 4, :] = entry[:, :LANES]
                pack[at + 4 : at + 8, :] = entry[:, LANES:]

    def readout(row, octets, piece):
        def one_group(g, carry):
            c = [
                [rows_c[row, s, half, g] for half in range(2)] for s in range(STEPS)
            ]
            for octet in octets:
                held = [jnp.zeros((8, LANES), jnp.float32) for _ in range(STEPS)]
                for p in range(DEPTH):
                    left, right = piece(GROUPS * p + g, octet)
                    for s in range(STEPS):
                        dot = jnp.sum(
                            left * c[s][0] + right * c[s][1], axis=1, keepdims=True
                        )
                        held[s] = jnp.where(lane == p, dot, held[s])
                for s in range(STEPS):
                    at = pl.multiple_of(g * PER_GROUP + octet * 8, 8)
                    dots[s, pl.ds(at, 8), :] = held[s]
            return carry

        lax.fori_loop(0, GROUPS, one_group, 0)

    def update(row, octets, piece):
        def one_group(g, carry):
            b = [[rows_b[row, s, half, g] for half in range(2)] for s in range(STEPS)]
            for octet in octets:
                heads = pl.ds(pl.multiple_of(g * PER_GROUP + octet * 8, 8), 8)

                def spread_out(at):
                    return jnp.broadcast_to(factors[row, heads, at : at + 1], (8, LANES))

                decay = spread_out(2 * DEPTH)
                for p in range(DEPTH):
                    u1 = spread_out(p)
                    u2 = spread_out(DEPTH + p)
                    k = GROUPS * p + g
                    for half, held in enumerate(piece(k, octet)):
                        final[
                            row,
                            k,
                            8 * octet : 8 * octet + 8,
                            half * LANES : (half + 1) * LANES,
                        ] = held * decay + u1 * b[0][half] + u2 * b[1][half]
            return carry

        lax.fori_loop(0, GROUPS, one_group, 0)

    def finish(row):
        for s in range(STEPS):
            dot = jnp.transpose(dots[s])[0:DEPTH, :]
            gated = (decays[row, s] * dot + extras[row, s]) * gates[row, s]
            at = Y_ROWS + (row * STEPS + s) * DEPTH
            pack[at : at + DEPTH, :] = gated
            sums[row * STEPS + s : row * STEPS + s + 1, :] = jnp.sum(
                gated * gated, axis=0, keepdims=True
            )

    prepare(
        0,
        kept_slot,
        [tail_x[kept, k].astype(jnp.float32) for k in range(3)],
        [[tail_bc[kept, k, b].astype(jnp.float32) for b in range(2)] for k in range(3)],
    )
    sums[4:8, :] = jnp.zeros((4, LANES), jnp.float32)

    def kept_piece(at, octet):
        rows = state[kept, at, 8 * octet : 8 * octet + 8, :]
        return rows[:, :LANES], rows[:, LANES:]

    readout(0, range(PER_GROUP // 8), kept_piece)
    finish(0)
    update(0, range(PER_GROUP // 8), kept_piece)
    outs = [
        pltpu.make_async_copy(final.at[0], final_hbm.at[0], out_sem.at[0]),
        pltpu.make_async_copy(pack, pack_hbm, out_sem.at[1]),
    ] + [
        pltpu.make_async_copy(
            final.at[1, :, pl.ds(chunk * PART, PART), :],
            final_hbm.at[1, :, pl.ds(chunk * PART, PART), :],
            out_sem.at[2 + chunk],
        )
        for chunk in range(CHUNKS)
    ] + [pltpu.make_async_copy(sums, sums_hbm.at[0], out_sem.at[2 + CHUNKS])]
    outs[0].start()

    def giver(to):
        from_low = lax.shift_right_logical(source[2 * to], 1)
        from_high = lax.shift_right_logical(source[2 * to + 1], 1)
        return jnp.where(from_low != to, from_low, from_high)

    for chunk in range(CHUNKS):
        all_pieces(0, chunk).wait_recv()

        def forward(i, carry, chunk=chunk):
            to = partner_of(me, i, devices)
            second[chunk][to] = spread[chunk][giver(to)]
            remote(1, chunk, to).start()
            return carry

        lax.fori_loop(1, devices, forward, 0)
        back[chunk][me] = spread[chunk][giver(me)]

    for chunk in range(CHUNKS):
        all_pieces(1, chunk).wait_recv()
        if chunk == 0:

            def untail(k, carry):
                tails[k, :] = back_a[k, 2 * PART, :]
                return carry

            lax.fori_loop(0, devices, untail, 0)
            quarter[...] = tails[TAIL_X_ROWS : TAIL_X_ROWS + 16, :]
            quarters[column] = quarter[...]
            shares = [
                pltpu.make_async_remote_copy(
                    src_ref=quarter,
                    dst_ref=quarters.at[column],
                    send_sem=share_send_sem.at[j - 1],
                    recv_sem=share_recv_sem.at[j - 1],
                    device_id={"tp": lax.rem(column + j, TP)},
                    device_id_type=MESH,
                )
                for j in range(1, TP)
            ]
            for copy in shares:
                copy.start()
            for copy in shares:
                copy.wait()
            for r in range(TAIL_X_ROWS):
                at = TAIL_X_ROWS + r
                tails[at : at + 1, :] = quarters[r // share, r % share : r % share + 1, :]
            window_bc = [
                [
                    jnp.concatenate(
                        [
                            tails[48 + (2 * k + b) * 8 : 52 + (2 * k + b) * 8, :],
                            tails[52 + (2 * k + b) * 8 : 56 + (2 * k + b) * 8, :],
                        ],
                        axis=1,
                    )
                    for b in range(2)
                ]
                for k in range(3)
            ]
            prepare(
                1,
                moved_slot,
                [tails[DEPTH * k : DEPTH * (k + 1), :] for k in range(3)],
                window_bc,
            )

        def moved_piece(at, octet, chunk=chunk):
            within = 8 * octet - PART * chunk
            return (
                back[chunk][at, within : within + 8, :],
                back[chunk][at, PART + within : PART + within + 8, :],
            )

        octets = range(chunk * PART // 8, (chunk + 1) * PART // 8)
        readout(1, octets, moved_piece)
        if chunk < CHUNKS - 1:
            update(1, octets, moved_piece)
            outs[2 + chunk].start()
    finish(1)

    exchanges = [
        pltpu.make_async_remote_copy(
            src_ref=sums,
            dst_ref=sums_hbm.at[j],
            send_sem=sum_send_sem.at[j - 1],
            recv_sem=sum_recv_sem.at[j - 1],
            device_id={"tp": lax.rem(column + j, TP)},
            device_id_type=MESH,
        )
        for j in range(1, TP)
    ]
    for exchange in exchanges:
        exchange.start()
    for at in (1, 2 + CHUNKS):
        outs[at].start()
    update(1, octets, moved_piece)
    outs[1 + CHUNKS].start()
    for exchange in exchanges:
        exchange.wait_recv()
    for exchange in exchanges:
        exchange.wait_send()
    for phase in range(2):
        for chunk in range(CHUNKS):
            all_pieces(phase, chunk).wait_send()
    for out in outs:
        out.wait()


PARTS = 2


def place_kernel(
    devices,
    source_hbm,
    active_hbm,
    norm_gain_hbm,
    sums_hbm,
    final_hbm,
    pack_hbm,
    state_out,
    tail_x_out,
    tail_bc_out,
    y_out,
    source,
    active,
    norm_gain,
    sums,
    held,
    pack,
    tail_x,
    tail_bc,
    y,
    sem,
    part_sem,
):
    me = lax.axis_index("rows")
    size = devices // PARTS
    source_load = pltpu.make_async_copy(source_hbm, source, sem.at[0])
    small_loads = [
        pltpu.make_async_copy(hbm, vmem, sem.at[1 + i])
        for i, (hbm, vmem) in enumerate(
            (
                (sums_hbm, sums),
                (pack_hbm, pack),
                (active_hbm, active),
                (norm_gain_hbm, norm_gain),
            )
        )
    ]
    source_load.start()
    for load in small_loads:
        load.start()
    parts = [(row, q) for row in range(2) for q in range(PARTS)]
    loads = [
        pltpu.make_async_copy(
            final_hbm.at[row, pl.ds(q * size, size)],
            held.at[row, pl.ds(q * size, size)],
            part_sem.at[row, q],
        )
        for row, q in parts
    ]
    for load in loads:
        load.start()
    source_load.wait()
    low = source[2 * me]
    high = source[2 * me + 1]
    kept = 1 - given_of(low, high, me)
    kept_slot = jnp.where(low == 2 * me + kept, 0, 1)
    slots = (kept_slot, 1 - kept_slot)
    writes = []
    for load, (row, q) in zip(loads, parts):
        load.wait()
        write = pltpu.make_async_copy(
            held.at[row, pl.ds(q * size, size)],
            state_out.at[slots[row], pl.ds(q * size, size)],
            part_sem.at[2 + row, q],
        )
        write.start()
        writes.append(write)
    for load in small_loads:
        load.wait()
    same_group = (
        lax.broadcasted_iota(jnp.int32, (LANES, LANES), 0) // PER_GROUP
        == lax.broadcasted_iota(jnp.int32, (LANES, LANES), 1) // PER_GROUP
    ).astype(jnp.float32)
    totals = jnp.dot(
        sums[0] + sums[1] + sums[2] + sums[3],
        same_group,
        preferred_element_type=jnp.float32,
        precision=lax.Precision.HIGHEST,
    )
    factor = lax.rsqrt(totals / (DEPTH * TP * PER_GROUP) + EPSILON)
    for row, slot in enumerate(slots):
        live = active[slot] == 1
        for s in range(STEPS):
            scale = factor[row * STEPS + s : row * STEPS + s + 1, :]
            at = Y_ROWS + (row * STEPS + s) * DEPTH
            scaled = pack[at : at + DEPTH, :] * scale * norm_gain[...]
            y[s, slot] = jnp.where(live, scaled, 0.0).astype(jnp.bfloat16)
        for k in range(3):
            at = TAIL_X + (row * 3 + k) * DEPTH
            tail_x[slot, k] = pack[at : at + DEPTH, :].astype(jnp.bfloat16)
            for c in range(2):
                at = TAIL_BC + ((row * 3 + k) * 2 + c) * 8
                tail_bc[slot, k, c] = jnp.concatenate(
                    [pack[at : at + 4, :], pack[at + 4 : at + 8, :]], axis=1
                ).astype(jnp.bfloat16)
    for i, (vmem, hbm) in enumerate(((tail_x, tail_x_out), (tail_bc, tail_bc_out), (y, y_out))):
        write = pltpu.make_async_copy(vmem, hbm, sem.at[5 + i])
        write.start()
        writes.append(write)
    for write in writes:
        write.wait()


def on_device(
    state_in,
    tail_x,
    tail_bc,
    source,
    active,
    x_new,
    z_new,
    bc_new,
    dt_new,
    conv_wx,
    conv_bx,
    conv_wbc,
    conv_bbc,
    dt_bias,
    a_log,
    skip_d,
    norm_gain,
):
    devices = lax.axis_size("rows")
    slots, depth, head_count, width = state_in.shape
    pieces = state_in.reshape(slots, devices, PER_GROUP, width)
    operands = (
        source,
        active,
        pieces,
        tail_x,
        tail_bc,
        x_new,
        z_new,
        bc_new,
        dt_new,
        conv_wx,
        conv_bx,
        conv_wbc,
        conv_bbc,
        dt_bias.reshape(1, -1),
        a_log.reshape(1, -1),
        skip_d.reshape(1, -1),
    )
    long_buffer = pltpu.VMEM((devices, 2 * PART + 1, LANES), jnp.float32)
    short_buffer = pltpu.VMEM((devices, 2 * PART, LANES), jnp.float32)
    hbm = pl.BlockSpec(memory_space=pltpu.HBM)
    final, pack, sums = pl.pallas_call(
        functools.partial(relocate_kernel, devices),
        out_shape=(
            jax.ShapeDtypeStruct(pieces.shape, jnp.float32),
            jax.ShapeDtypeStruct((PACK_ROWS, LANES), jnp.float32),
            jax.ShapeDtypeStruct((TP, 8, LANES), jnp.float32),
        ),
        in_specs=[hbm] * len(operands),
        out_specs=(hbm, hbm, hbm),
        scratch_shapes=[
            pltpu.SMEM(source.shape, jnp.int32),
            pltpu.SMEM(active.shape, jnp.int32),
        ]
        + [pltpu.VMEM(a.shape, a.dtype) for a in operands[2:]]
        + [
            pltpu.VMEM((2 * TAIL_X_ROWS, LANES), jnp.float32),
            pltpu.VMEM((16, LANES), jnp.float32),
            pltpu.VMEM((TP, 16, LANES), jnp.float32),
        ]
        + [long_buffer, short_buffer] * 4
        + [
            pltpu.VMEM((PACK_ROWS, LANES), jnp.float32),
            pltpu.VMEM(pieces.shape, jnp.float32),
            pltpu.VMEM((2, STEPS, 2, GROUPS, 8, LANES), jnp.float32),
            pltpu.VMEM((2, STEPS, 2, GROUPS, 8, LANES), jnp.float32),
            pltpu.VMEM((2, LANES, LANES), jnp.float32),
            pltpu.VMEM((2, STEPS, DEPTH, LANES), jnp.float32),
            pltpu.VMEM((2, STEPS, DEPTH, LANES), jnp.float32),
            pltpu.VMEM((2, STEPS, DEPTH, LANES), jnp.float32),
            pltpu.VMEM((STEPS, LANES, LANES), jnp.float32),
            pltpu.VMEM((LANES, LANES), jnp.float32),
            pltpu.VMEM((8, LANES), jnp.float32),
            pltpu.SemaphoreType.DMA((len(operands),)),
            pltpu.SemaphoreType.DMA((2, CHUNKS)),
            pltpu.SemaphoreType.DMA((2, CHUNKS)),
            pltpu.SemaphoreType.DMA((TP - 1,)),
            pltpu.SemaphoreType.DMA((TP - 1,)),
            pltpu.SemaphoreType.DMA((TP - 1,)),
            pltpu.SemaphoreType.DMA((TP - 1,)),
            pltpu.SemaphoreType.DMA((3 + CHUNKS,)),
        ],
        compiler_params=pltpu.CompilerParams(
            collective_id=0, has_side_effects=True, vmem_limit_bytes=60 * 1024 * 1024
        ),
    )(*operands)
    state, window_x, window_bc, y = pl.pallas_call(
        functools.partial(place_kernel, devices),
        out_shape=(
            jax.ShapeDtypeStruct(pieces.shape, jnp.float32),
            jax.ShapeDtypeStruct(tail_x.shape, tail_x.dtype),
            jax.ShapeDtypeStruct(tail_bc.shape, tail_bc.dtype),
            jax.ShapeDtypeStruct(x_new.shape, jnp.bfloat16),
        ),
        in_specs=[hbm] * 6,
        out_specs=(hbm,) * 4,
        scratch_shapes=[
            pltpu.SMEM(source.shape, jnp.int32),
            pltpu.SMEM(active.shape, jnp.int32),
            pltpu.VMEM(norm_gain.shape, jnp.float32),
            pltpu.VMEM((TP, 8, LANES), jnp.float32),
            pltpu.VMEM(pieces.shape, jnp.float32),
            pltpu.VMEM((PACK_ROWS, LANES), jnp.float32),
            pltpu.VMEM(tail_x.shape, tail_x.dtype),
            pltpu.VMEM(tail_bc.shape, tail_bc.dtype),
            pltpu.VMEM(x_new.shape, jnp.bfloat16),
            pltpu.SemaphoreType.DMA((8,)),
            pltpu.SemaphoreType.DMA((4, PARTS)),
        ],
        compiler_params=pltpu.CompilerParams(vmem_limit_bytes=60 * 1024 * 1024),
    )(source, active, norm_gain, sums, final, pack)
    return state.reshape(state_in.shape), window_x, window_bc, y


def solution(mesh):
    return jax.shard_map(
        on_device,
        mesh=mesh,
        in_specs=(
            P("rows", "tp", None, None),
            P("rows", None, "tp", None),
            P("rows", None, None, None, None),
            P(),
            P("rows"),
            P(None, "rows", "tp", None),
            P(None, "rows", "tp", None),
            P(None, "rows", None, None, None),
            P(None, "rows", None),
            P(None, "tp", None),
            P("tp", None),
            P(),
            P(),
            P(),
            P(),
            P(),
            P("tp", None),
        ),
        out_specs=(
            P("rows", "tp", None, None),
            P("rows", None, "tp", None),
            P("rows", None, None, None, None),
            P(None, "rows", "tp", None),
        ),
        check_vma=False,
    )
```

```python
import functools
import jax
import jax.numpy as jnp
from jax import lax
from jax.experimental import pallas as pl
from jax.experimental.pallas import tpu as pltpu
from jax.sharding import PartitionSpec as P

STEPS = 2
EPSILON = 1e-05
MESH = pl.DeviceIdType.MESH
CHUNKS = 2
TAIL_X_ROWS = 48
LANES = 128
DEPTH = 16
GROUPS = 4
PER_GROUP = 32
PART = PER_GROUP // CHUNKS
TP = 4

Y_ROWS = 0
TAIL_X = 64
TAIL_BC = 160
PACK_ROWS = 256


def silu(v):
    return v / (1.0 + jnp.exp(-v))


def partner_of(me, i, devices):
    return lax.rem(me + i, devices)


def given_of(low, high, me):
    return jnp.where((low != 2 * me) & (high != 2 * me), 0, 1)


def relocate_kernel(
    devices,
    source_hbm,
    active_hbm,
    state_hbm,
    tail_x_hbm,
    tail_bc_hbm,
    x_new_hbm,
    z_new_hbm,
    bc_new_hbm,
    dt_new_hbm,
    conv_wx_hbm,
    conv_bx_hbm,
    conv_wbc_hbm,
    conv_bbc_hbm,
    dt_bias_hbm,
    a_log_hbm,
    skip_d_hbm,
    final_hbm,
    pack_hbm,
    sums_hbm,
    source,
    active,
    state,
    tail_x,
    tail_bc,
    x_new,
    z_new,
    bc_new,
    dt_new,
    conv_wx,
    conv_bx,
    conv_wbc,
    conv_bbc,
    dt_bias,
    a_log,
    skip_d,
    tails,
    quarter,
    quarters,
    first_a,
    first_b,
    spread_a,
    spread_b,
    second_a,
    second_b,
    back_a,
    back_b,
    pack,
    final,
    rows_b,
    rows_c,
    factors,
    decays,
    extras,
    gates,
    dots,
    turned,
    sums,
    load_sem,
    send_sem,
    recv_sem,
    sum_send_sem,
    sum_recv_sem,
    share_send_sem,
    share_recv_sem,
    out_sem,
):
    me = lax.axis_index("rows")
    column = lax.axis_index("tp")
    first, spread, second, back = (
        (first_a, first_b),
        (spread_a, spread_b),
        (second_a, second_b),
        (back_a, back_b),
    )
    loads = [
        pltpu.make_async_copy(src, dst, load_sem.at[i])
        for i, (src, dst) in enumerate(
            (
                (source_hbm, source),
                (tail_x_hbm, tail_x),
                (tail_bc_hbm, tail_bc),
                (state_hbm, state),
                (active_hbm, active),
                (x_new_hbm, x_new),
                (z_new_hbm, z_new),
                (bc_new_hbm, bc_new),
                (dt_new_hbm, dt_new),
                (conv_wx_hbm, conv_wx),
                (conv_bx_hbm, conv_bx),
                (conv_wbc_hbm, conv_wbc),
                (conv_bbc_hbm, conv_bbc),
                (dt_bias_hbm, dt_bias),
                (a_log_hbm, a_log),
                (skip_d_hbm, skip_d),
            )
        )
    ]
    for load in loads[:4]:
        load.start()
    barrier = pltpu.get_barrier_semaphore()

    def greet(i, carry):
        pl.semaphore_signal(
            barrier,
            inc=1,
            device_id={"rows": partner_of(me, i, devices)},
            device_id_type=MESH,
        )
        return carry

    lax.fori_loop(1, devices, greet, 0)
    for j in range(1, TP):
        pl.semaphore_signal(
            barrier,
            inc=1,
            device_id={"tp": lax.rem(column + j, TP)},
            device_id_type=MESH,
        )

    for load in loads[4:]:
        load.start()
    loads[0].wait()
    low = source[2 * me]
    high = source[2 * me + 1]
    given = given_of(low, high, me)
    kept = 1 - given
    kept_slot = jnp.where(low == 2 * me + kept, 0, 1)
    moved_slot = 1 - kept_slot

    loads[1].wait()
    loads[2].wait()
    for k in range(3):
        tails[DEPTH * k : DEPTH * (k + 1), :] = tail_x[given, k].astype(jnp.float32)
        for b in range(2):
            entry = tail_bc[given, k, b].astype(jnp.float32)
            at = 48 + (2 * k + b) * 8
            tails[at : at + 4, :] = entry[:, :LANES]
            tails[at + 4 : at + 8, :] = entry[:, LANES:]

    def remote(phase, chunk, to):
        source_ref, target_ref = ((first, spread), (second, back))[phase]
        return pltpu.make_async_remote_copy(
            src_ref=source_ref[chunk].at[to],
            dst_ref=target_ref[chunk].at[me],
            send_sem=send_sem.at[phase, chunk],
            recv_sem=recv_sem.at[phase, chunk],
            device_id={"rows": to},
            device_id_type=MESH,
        )

    def all_pieces(phase, chunk):
        source_ref, target_ref = ((first, spread), (second, back))[phase]
        return pltpu.make_async_remote_copy(
            src_ref=source_ref[chunk].at[pl.ds(0, devices - 1)],
            dst_ref=target_ref[chunk].at[pl.ds(0, devices - 1)],
            send_sem=send_sem.at[phase, chunk],
            recv_sem=recv_sem.at[phase, chunk],
            device_id={"rows": partner_of(me, 1, devices)},
            device_id_type=MESH,
        )

    share = TAIL_X_ROWS // TP

    def fill(chunk, piece, into, at):
        rows = state[given, piece, chunk * PART : (chunk + 1) * PART, :]
        into[at, 0:PART, :] = rows[:, :LANES]
        into[at, PART : 2 * PART, :] = rows[:, LANES:]
        if chunk == 0:
            entry = TAIL_X_ROWS + share * column + lax.rem(piece, share)
            into[at, 2 * PART, :] = tails[jnp.where(piece < TAIL_X_ROWS, piece, entry), :]

    def ready(chunk):
        def one(i, carry):
            to = partner_of(me, i, devices)
            fill(chunk, to, first[chunk], to)
            return carry

        lax.fori_loop(1, devices, one, 0)
        fill(chunk, me, spread[chunk], me)

    loads[3].wait()
    for chunk in range(CHUNKS):
        ready(chunk)
    pl.semaphore_wait(barrier, devices - 1 + TP - 1)
    for chunk in range(CHUNKS):

        def begin(i, carry, chunk=chunk):
            remote(0, chunk, partner_of(me, i, devices)).start()
            return carry

        lax.fori_loop(1, devices, begin, 0)

    for load in loads[4:]:
        load.wait()
    group_of_lane = lax.broadcasted_iota(jnp.int32, (GROUPS, LANES), 1) // PER_GROUP
    own_group = group_of_lane == lax.broadcasted_iota(jnp.int32, (GROUPS, LANES), 0)
    lane = lax.broadcasted_iota(jnp.int32, (8, LANES), 1)

    def by_head(values):
        return jnp.sum(jnp.where(own_group, values, 0.0), axis=0, keepdims=True)

    def prepare(row, slot, window_x, window_bc):
        live = active[slot] == 1
        new_x = [x_new[s, slot].astype(jnp.float32) for s in range(STEPS)]
        new_bc = [
            [bc_new[s, slot, b].astype(jnp.float32) for b in range(2)] for s in range(STEPS)
        ]
        frames_x = window_x + new_x
        frames_bc = window_bc + new_bc
        conv_x = []
        conv_b = []
        conv_c = []
        sizes = []
        decay = []
        rate = jnp.exp(a_log[...])
        for s in range(STEPS):
            total = frames_x[s] * conv_wx[0]
            for k in range(1, 4):
                total = total + frames_x[s + k] * conv_wx[k]
            conv_x.append(silu(total + conv_bx[...]))
            pair = []
            for b in range(2):
                total = frames_bc[s][b] * conv_wbc[0, b]
                for k in range(1, 4):
                    total = total + frames_bc[s + k][b] * conv_wbc[k, b]
                pair.append(silu(total + conv_bbc[b]))
            conv_b.append(pair[0])
            conv_c.append(pair[1])
            raw = jnp.where(slot == 0, dt_new[s, 0:1, :], dt_new[s, 1:2, :]) + dt_bias[...]
            size = jnp.maximum(raw, 0.0) + jnp.log1p(jnp.exp(-jnp.abs(raw)))
            sizes.append(size)
            decay.append(jnp.exp(-size * rate))
            for half in range(2):
                for g in range(GROUPS):
                    at = slice(half * LANES, (half + 1) * LANES)
                    rows_b[row, s, half, g] = jnp.broadcast_to(pair[0][g : g + 1, at], (8, LANES))
                    rows_c[row, s, half, g] = jnp.broadcast_to(pair[1][g : g + 1, at], (8, LANES))
            gates[row, s] = silu(z_new[s, slot].astype(jnp.float32))

        def overlap(i, j):
            return by_head(jnp.sum(conv_b[i] * conv_c[j], axis=1, keepdims=True))

        skip = skip_d[...]
        put_in = [sizes[s] * conv_x[s] for s in range(STEPS)]
        carried = put_in[0] * decay[1]
        both = decay[0] * decay[1]
        decays[row, 0] = jnp.broadcast_to(decay[0], (DEPTH, LANES))
        decays[row, 1] = jnp.broadcast_to(both, (DEPTH, LANES))
        extras[row, 0] = put_in[0] * overlap(0, 0) + skip * conv_x[0]
        extras[row, 1] = (
            carried * overlap(0, 1) + put_in[1] * overlap(1, 1) + skip * conv_x[1]
        )
        turned[0:DEPTH, :] = jnp.where(live, carried, 0.0)
        turned[DEPTH : 2 * DEPTH, :] = jnp.where(live, put_in[1], 0.0)
        turned[2 * DEPTH : 2 * DEPTH + 8, :] = jnp.broadcast_to(
            jnp.where(live, both, 1.0), (8, LANES)
        )
        turned[2 * DEPTH + 8 :, :] = jnp.zeros((LANES - 2 * DEPTH - 8, LANES), jnp.float32)
        factors[row] = jnp.transpose(turned[...])
        for k in range(3):
            at = TAIL_X + (row * 3 + k) * DEPTH
            pack[at : at + DEPTH, :] = jnp.where(live, frames_x[k + 2], frames_x[k])
            for b in range(2):
                entry = jnp.where(live, frames_bc[k + 2][b], frames_bc[k][b])
                at = TAIL_BC + ((row * 3 + k) * 2 + b) * 8
                pack[at : at + 4, :] = entry[:, :LANES]
                pack[at + 4 : at + 8, :] = entry[:, LANES:]

    def readout(row, octets, piece):
        def one_group(g, carry):
            c = [
                [rows_c[row, s, half, g] for half in range(2)] for s in range(STEPS)
            ]
            for octet in octets:
                held = [jnp.zeros((8, LANES), jnp.float32) for _ in range(STEPS)]
                for p in range(DEPTH):
                    left, right = piece(GROUPS * p + g, octet)
                    for s in range(STEPS):
                        dot = jnp.sum(
                            left * c[s][0] + right * c[s][1], axis=1, keepdims=True
                        )
                        held[s] = jnp.where(lane == p, dot, held[s])
                for s in range(STEPS):
                    at = pl.multiple_of(g * PER_GROUP + octet * 8, 8)
                    dots[s, pl.ds(at, 8), :] = held[s]
            return carry

        lax.fori_loop(0, GROUPS, one_group, 0)

    def update(row, octets, piece):
        def one_group(g, carry):
            b = [[rows_b[row, s, half, g] for half in range(2)] for s in range(STEPS)]
            for octet in octets:
                heads = pl.ds(pl.multiple_of(g * PER_GROUP + octet * 8, 8), 8)

                def spread_out(at):
                    return jnp.broadcast_to(factors[row, heads, at : at + 1], (8, LANES))

                decay = spread_out(2 * DEPTH)
                for p in range(DEPTH):
                    u1 = spread_out(p)
                    u2 = spread_out(DEPTH + p)
                    k = GROUPS * p + g
                    for half, held in enumerate(piece(k, octet)):
                        final[
                            row,
                            k,
                            8 * octet : 8 * octet + 8,
                            half * LANES : (half + 1) * LANES,
                        ] = held * decay + u1 * b[0][half] + u2 * b[1][half]
            return carry

        lax.fori_loop(0, GROUPS, one_group, 0)

    def finish(row):
        for s in range(STEPS):
            dot = jnp.transpose(dots[s])[0:DEPTH, :]
            gated = (decays[row, s] * dot + extras[row, s]) * gates[row, s]
            at = Y_ROWS + (row * STEPS + s) * DEPTH
            pack[at : at + DEPTH, :] = gated
            sums[row * STEPS + s : row * STEPS + s + 1, :] = jnp.sum(
                gated * gated, axis=0, keepdims=True
            )

    prepare(
        0,
        kept_slot,
        [tail_x[kept, k].astype(jnp.float32) for k in range(3)],
        [[tail_bc[kept, k, b].astype(jnp.float32) for b in range(2)] for k in range(3)],
    )
    sums[4:8, :] = jnp.zeros((4, LANES), jnp.float32)

    def kept_piece(at, octet):
        rows = state[kept, at, 8 * octet : 8 * octet + 8, :]
        return rows[:, :LANES], rows[:, LANES:]

    readout(0, range(PER_GROUP // 8), kept_piece)
    finish(0)
    update(0, range(PER_GROUP // 8), kept_piece)
    outs = [
        pltpu.make_async_copy(final.at[0], final_hbm.at[0], out_sem.at[0]),
        pltpu.make_async_copy(pack, pack_hbm, out_sem.at[1]),
    ] + [
        pltpu.make_async_copy(
            final.at[1, :, pl.ds(chunk * PART, PART), :],
            final_hbm.at[1, :, pl.ds(chunk * PART, PART), :],
            out_sem.at[2 + chunk],
        )
        for chunk in range(CHUNKS)
    ] + [pltpu.make_async_copy(sums, sums_hbm.at[0], out_sem.at[2 + CHUNKS])]
    outs[0].start()

    def giver(to):
        from_low = lax.shift_right_logical(source[2 * to], 1)
        from_high = lax.shift_right_logical(source[2 * to + 1], 1)
        return jnp.where(from_low != to, from_low, from_high)

    for chunk in range(CHUNKS):
        all_pieces(0, chunk).wait_recv()

        def forward(i, carry, chunk=chunk):
            to = partner_of(me, i, devices)
            second[chunk][to] = spread[chunk][giver(to)]
            remote(1, chunk, to).start()
            return carry

        lax.fori_loop(1, devices, forward, 0)
        back[chunk][me] = spread[chunk][giver(me)]

    for chunk in range(CHUNKS):
        all_pieces(1, chunk).wait_recv()
        if chunk == 0:

            def untail(k, carry):
                tails[k, :] = back_a[k, 2 * PART, :]
                return carry

            lax.fori_loop(0, devices, untail, 0)
            quarter[...] = tails[TAIL_X_ROWS : TAIL_X_ROWS + 16, :]
            quarters[column] = quarter[...]
            shares = [
                pltpu.make_async_remote_copy(
                    src_ref=quarter,
                    dst_ref=quarters.at[column],
                    send_sem=share_send_sem.at[j - 1],
                    recv_sem=share_recv_sem.at[j - 1],
                    device_id={"tp": lax.rem(column + j, TP)},
                    device_id_type=MESH,
                )
                for j in range(1, TP)
            ]
            for copy in shares:
                copy.start()
            for copy in shares:
                copy.wait()
            for r in range(TAIL_X_ROWS):
                at = TAIL_X_ROWS + r
                tails[at : at + 1, :] = quarters[r // share, r % share : r % share + 1, :]
            window_bc = [
                [
                    jnp.concatenate(
                        [
                            tails[48 + (2 * k + b) * 8 : 52 + (2 * k + b) * 8, :],
                            tails[52 + (2 * k + b) * 8 : 56 + (2 * k + b) * 8, :],
                        ],
                        axis=1,
                    )
                    for b in range(2)
                ]
                for k in range(3)
            ]
            prepare(
                1,
                moved_slot,
                [tails[DEPTH * k : DEPTH * (k + 1), :] for k in range(3)],
                window_bc,
            )

        def moved_piece(at, octet, chunk=chunk):
            within = 8 * octet - PART * chunk
            return (
                back[chunk][at, within : within + 8, :],
                back[chunk][at, PART + within : PART + within + 8, :],
            )

        octets = range(chunk * PART // 8, (chunk + 1) * PART // 8)
        readout(1, octets, moved_piece)
        if chunk < CHUNKS - 1:
            update(1, octets, moved_piece)
            outs[2 + chunk].start()
    finish(1)

    exchanges = [
        pltpu.make_async_remote_copy(
            src_ref=sums,
            dst_ref=sums_hbm.at[j],
            send_sem=sum_send_sem.at[j - 1],
            recv_sem=sum_recv_sem.at[j - 1],
            device_id={"tp": lax.rem(column + j, TP)},
            device_id_type=MESH,
        )
        for j in range(1, TP)
    ]
    for exchange in exchanges:
        exchange.start()
    for at in (1, 2 + CHUNKS):
        outs[at].start()
    update(1, octets, moved_piece)
    outs[1 + CHUNKS].start()
    for exchange in exchanges:
        exchange.wait_recv()
    for exchange in exchanges:
        exchange.wait_send()
    for phase in range(2):
        for chunk in range(CHUNKS):
            all_pieces(phase, chunk).wait_send()
    for out in outs:
        out.wait()


PARTS = 2


def place_kernel(
    devices,
    source_hbm,
    active_hbm,
    norm_gain_hbm,
    sums_hbm,
    final_hbm,
    pack_hbm,
    state_out,
    tail_x_out,
    tail_bc_out,
    y_out,
    source,
    active,
    norm_gain,
    sums,
    held,
    pack,
    tail_x,
    tail_bc,
    y,
    sem,
    part_sem,
):
    me = lax.axis_index("rows")
    size = devices // PARTS
    source_load = pltpu.make_async_copy(source_hbm, source, sem.at[0])
    small_loads = [
        pltpu.make_async_copy(hbm, vmem, sem.at[1 + i])
        for i, (hbm, vmem) in enumerate(
            (
                (sums_hbm, sums),
                (pack_hbm, pack),
                (active_hbm, active),
                (norm_gain_hbm, norm_gain),
            )
        )
    ]
    source_load.start()
    for load in small_loads:
        load.start()
    parts = [(row, q) for row in range(2) for q in range(PARTS)]
    loads = [
        pltpu.make_async_copy(
            final_hbm.at[row, pl.ds(q * size, size)],
            held.at[row, pl.ds(q * size, size)],
            part_sem.at[row, q],
        )
        for row, q in parts
    ]
    for load in loads:
        load.start()
    source_load.wait()
    low = source[2 * me]
    high = source[2 * me + 1]
    kept = 1 - given_of(low, high, me)
    kept_slot = jnp.where(low == 2 * me + kept, 0, 1)
    slots = (kept_slot, 1 - kept_slot)
    writes = []
    for load, (row, q) in zip(loads, parts):
        load.wait()
        write = pltpu.make_async_copy(
            held.at[row, pl.ds(q * size, size)],
            state_out.at[slots[row], pl.ds(q * size, size)],
            part_sem.at[2 + row, q],
        )
        write.start()
        writes.append(write)
    for load in small_loads:
        load.wait()
    same_group = (
        lax.broadcasted_iota(jnp.int32, (LANES, LANES), 0) // PER_GROUP
        == lax.broadcasted_iota(jnp.int32, (LANES, LANES), 1) // PER_GROUP
    ).astype(jnp.float32)
    totals = jnp.dot(
        sums[0] + sums[1] + sums[2] + sums[3],
        same_group,
        preferred_element_type=jnp.float32,
        precision=lax.Precision.HIGHEST,
    )
    factor = lax.rsqrt(totals / (DEPTH * TP * PER_GROUP) + EPSILON)
    for row, slot in enumerate(slots):
        live = active[slot] == 1
        for s in range(STEPS):
            scale = factor[row * STEPS + s : row * STEPS + s + 1, :]
            at = Y_ROWS + (row * STEPS + s) * DEPTH
            scaled = pack[at : at + DEPTH, :] * scale * norm_gain[...]
            y[s, slot] = jnp.where(live, scaled, 0.0).astype(jnp.bfloat16)
        for k in range(3):
            at = TAIL_X + (row * 3 + k) * DEPTH
            tail_x[slot, k] = pack[at : at + DEPTH, :].astype(jnp.bfloat16)
            for c in range(2):
                at = TAIL_BC + ((row * 3 + k) * 2 + c) * 8
                tail_bc[slot, k, c] = jnp.concatenate(
                    [pack[at : at + 4, :], pack[at + 4 : at + 8, :]], axis=1
                ).astype(jnp.bfloat16)
    for i, (vmem, hbm) in enumerate(((tail_x, tail_x_out), (tail_bc, tail_bc_out), (y, y_out))):
        write = pltpu.make_async_copy(vmem, hbm, sem.at[5 + i])
        write.start()
        writes.append(write)
    for write in writes:
        write.wait()


def on_device(
    state_in,
    tail_x,
    tail_bc,
    source,
    active,
    x_new,
    z_new,
    bc_new,
    dt_new,
    conv_wx,
    conv_bx,
    conv_wbc,
    conv_bbc,
    dt_bias,
    a_log,
    skip_d,
    norm_gain,
):
    devices = lax.axis_size("rows")
    slots, depth, head_count, width = state_in.shape
    pieces = state_in.reshape(slots, devices, PER_GROUP, width)
    operands = (
        source,
        active,
        pieces,
        tail_x,
        tail_bc,
        x_new,
        z_new,
        bc_new,
        dt_new,
        conv_wx,
        conv_bx,
        conv_wbc,
        conv_bbc,
        dt_bias.reshape(1, -1),
        a_log.reshape(1, -1),
        skip_d.reshape(1, -1),
    )
    long_buffer = pltpu.VMEM((devices, 2 * PART + 1, LANES), jnp.float32)
    short_buffer = pltpu.VMEM((devices, 2 * PART, LANES), jnp.float32)
    hbm = pl.BlockSpec(memory_space=pltpu.HBM)
    final, pack, sums = pl.pallas_call(
        functools.partial(relocate_kernel, devices),
        out_shape=(
            jax.ShapeDtypeStruct(pieces.shape, jnp.float32),
            jax.ShapeDtypeStruct((PACK_ROWS, LANES), jnp.float32),
            jax.ShapeDtypeStruct((TP, 8, LANES), jnp.float32),
        ),
        in_specs=[hbm] * len(operands),
        out_specs=(hbm, hbm, hbm),
        scratch_shapes=[
            pltpu.SMEM(source.shape, jnp.int32),
            pltpu.SMEM(active.shape, jnp.int32),
        ]
        + [pltpu.VMEM(a.shape, a.dtype) for a in operands[2:]]
        + [
            pltpu.VMEM((2 * TAIL_X_ROWS, LANES), jnp.float32),
            pltpu.VMEM((16, LANES), jnp.float32),
            pltpu.VMEM((TP, 16, LANES), jnp.float32),
        ]
        + [long_buffer, short_buffer] * 4
        + [
            pltpu.VMEM((PACK_ROWS, LANES), jnp.float32),
            pltpu.VMEM(pieces.shape, jnp.float32),
            pltpu.VMEM((2, STEPS, 2, GROUPS, 8, LANES), jnp.float32),
            pltpu.VMEM((2, STEPS, 2, GROUPS, 8, LANES), jnp.float32),
            pltpu.VMEM((2, LANES, LANES), jnp.float32),
            pltpu.VMEM((2, STEPS, DEPTH, LANES), jnp.float32),
            pltpu.VMEM((2, STEPS, DEPTH, LANES), jnp.float32),
            pltpu.VMEM((2, STEPS, DEPTH, LANES), jnp.float32),
            pltpu.VMEM((STEPS, LANES, LANES), jnp.float32),
            pltpu.VMEM((LANES, LANES), jnp.float32),
            pltpu.VMEM((8, LANES), jnp.float32),
            pltpu.SemaphoreType.DMA((len(operands),)),
            pltpu.SemaphoreType.DMA((2, CHUNKS)),
            pltpu.SemaphoreType.DMA((2, CHUNKS)),
            pltpu.SemaphoreType.DMA((TP - 1,)),
            pltpu.SemaphoreType.DMA((TP - 1,)),
            pltpu.SemaphoreType.DMA((TP - 1,)),
            pltpu.SemaphoreType.DMA((TP - 1,)),
            pltpu.SemaphoreType.DMA((3 + CHUNKS,)),
        ],
        compiler_params=pltpu.CompilerParams(
            collective_id=0, has_side_effects=True, vmem_limit_bytes=60 * 1024 * 1024
        ),
    )(*operands)
    state, window_x, window_bc, y = pl.pallas_call(
        functools.partial(place_kernel, devices),
        out_shape=(
            jax.ShapeDtypeStruct(pieces.shape, jnp.float32),
            jax.ShapeDtypeStruct(tail_x.shape, tail_x.dtype),
            jax.ShapeDtypeStruct(tail_bc.shape, tail_bc.dtype),
            jax.ShapeDtypeStruct(x_new.shape, jnp.bfloat16),
        ),
        in_specs=[hbm] * 6,
        out_specs=(hbm,) * 4,
        scratch_shapes=[
            pltpu.SMEM(source.shape, jnp.int32),
            pltpu.SMEM(active.shape, jnp.int32),
            pltpu.VMEM(norm_gain.shape, jnp.float32),
            pltpu.VMEM((TP, 8, LANES), jnp.float32),
            pltpu.VMEM(pieces.shape, jnp.float32),
            pltpu.VMEM((PACK_ROWS, LANES), jnp.float32),
            pltpu.VMEM(tail_x.shape, tail_x.dtype),
            pltpu.VMEM(tail_bc.shape, tail_bc.dtype),
            pltpu.VMEM(x_new.shape, jnp.bfloat16),
            pltpu.SemaphoreType.DMA((8,)),
            pltpu.SemaphoreType.DMA((4, PARTS)),
        ],
        compiler_params=pltpu.CompilerParams(vmem_limit_bytes=60 * 1024 * 1024),
    )(source, active, norm_gain, sums, final, pack)
    return state.reshape(state_in.shape), window_x, window_bc, y


def solution(mesh):
    return jax.shard_map(
        on_device,
        mesh=mesh,
        in_specs=(
            P("rows", "tp", None, None),
            P("rows", None, "tp", None),
            P("rows", None, None, None, None),
            P(),
            P("rows"),
            P(None, "rows", "tp", None),
            P(None, "rows", "tp", None),
            P(None, "rows", None, None, None),
            P(None, "rows", None),
            P(None, "tp", None),
            P("tp", None),
            P(),
            P(),
            P(),
            P(),
            P(),
            P("tp", None),
        ),
        out_specs=(
            P("rows", "tp", None, None),
            P("rows", None, "tp", None),
            P("rows", None, None, None, None),
            P(None, "rows", "tp", None),
        ),
        check_vma=False,
    )
```

```python
import functools
import jax
import jax.numpy as jnp
from jax import lax
from jax.experimental import pallas as pl
from jax.experimental.pallas import tpu as pltpu
from jax.sharding import PartitionSpec as P

STEPS = 2
EPSILON = 1e-05
MESH = pl.DeviceIdType.MESH
CHUNKS = 2
TAIL_X_ROWS = 48
LANES = 128
DEPTH = 16
GROUPS = 4
PER_GROUP = 32
PART = PER_GROUP // CHUNKS
TP = 4

Y_ROWS = 0
TAIL_X = 64
TAIL_BC = 160
PACK_ROWS = 256


def silu(v):
    return v / (1.0 + jnp.exp(-v))


def partner_of(me, i, devices):
    return lax.rem(me + i, devices)


def given_of(low, high, me):
    return jnp.where((low != 2 * me) & (high != 2 * me), 0, 1)


def relocate_kernel(
    devices,
    source_hbm,
    active_hbm,
    state_hbm,
    tail_x_hbm,
    tail_bc_hbm,
    x_new_hbm,
    z_new_hbm,
    bc_new_hbm,
    dt_new_hbm,
    conv_wx_hbm,
    conv_bx_hbm,
    conv_wbc_hbm,
    conv_bbc_hbm,
    dt_bias_hbm,
    a_log_hbm,
    skip_d_hbm,
    final_hbm,
    pack_hbm,
    sums_hbm,
    source,
    active,
    state,
    tail_x,
    tail_bc,
    x_new,
    z_new,
    bc_new,
    dt_new,
    conv_wx,
    conv_bx,
    conv_wbc,
    conv_bbc,
    dt_bias,
    a_log,
    skip_d,
    tails,
    quarter,
    quarters,
    first_a,
    first_b,
    spread_a,
    spread_b,
    second_a,
    second_b,
    back_a,
    back_b,
    pack,
    final,
    rows_b,
    rows_c,
    factors,
    decays,
    extras,
    gates,
    dots,
    turned,
    sums,
    load_sem,
    send_sem,
    recv_sem,
    sum_send_sem,
    sum_recv_sem,
    share_send_sem,
    share_recv_sem,
    out_sem,
):
    me = lax.axis_index("rows")
    column = lax.axis_index("tp")
    first, spread, second, back = (
        (first_a, first_b),
        (spread_a, spread_b),
        (second_a, second_b),
        (back_a, back_b),
    )
    loads = [
        pltpu.make_async_copy(src, dst, load_sem.at[i])
        for i, (src, dst) in enumerate(
            (
                (source_hbm, source),
                (tail_x_hbm, tail_x),
                (tail_bc_hbm, tail_bc),
                (state_hbm, state),
                (active_hbm, active),
                (x_new_hbm, x_new),
                (z_new_hbm, z_new),
                (bc_new_hbm, bc_new),
                (dt_new_hbm, dt_new),
                (conv_wx_hbm, conv_wx),
                (conv_bx_hbm, conv_bx),
                (conv_wbc_hbm, conv_wbc),
                (conv_bbc_hbm, conv_bbc),
                (dt_bias_hbm, dt_bias),
                (a_log_hbm, a_log),
                (skip_d_hbm, skip_d),
            )
        )
    ]
    for load in loads[:4]:
        load.start()
    barrier = pltpu.get_barrier_semaphore()

    def greet(i, carry):
        pl.semaphore_signal(
            barrier,
            inc=1,
            device_id={"rows": partner_of(me, i, devices)},
            device_id_type=MESH,
        )
        return carry

    lax.fori_loop(1, devices, greet, 0)
    for j in range(1, TP):
        pl.semaphore_signal(
            barrier,
            inc=1,
            device_id={"tp": lax.rem(column + j, TP)},
            device_id_type=MESH,
        )

    for load in loads[4:]:
        load.start()
    loads[0].wait()
    low = source[2 * me]
    high = source[2 * me + 1]
    given = given_of(low, high, me)
    kept = 1 - given
    kept_slot = jnp.where(low == 2 * me + kept, 0, 1)
    moved_slot = 1 - kept_slot

    loads[1].wait()
    loads[2].wait()
    for k in range(3):
        tails[DEPTH * k : DEPTH * (k + 1), :] = tail_x[given, k].astype(jnp.float32)
        for b in range(2):
            entry = tail_bc[given, k, b].astype(jnp.float32)
            at = 48 + (2 * k + b) * 8
            tails[at : at + 4, :] = entry[:, :LANES]
            tails[at + 4 : at + 8, :] = entry[:, LANES:]

    def remote(phase, chunk, to):
        source_ref, target_ref = ((first, spread), (second, back))[phase]
        return pltpu.make_async_remote_copy(
            src_ref=source_ref[chunk].at[to],
            dst_ref=target_ref[chunk].at[me],
            send_sem=send_sem.at[phase, chunk],
            recv_sem=recv_sem.at[phase, chunk],
            device_id={"rows": to},
            device_id_type=MESH,
        )

    def all_pieces(phase, chunk):
        source_ref, target_ref = ((first, spread), (second, back))[phase]
        return pltpu.make_async_remote_copy(
            src_ref=source_ref[chunk].at[pl.ds(0, devices - 1)],
            dst_ref=target_ref[chunk].at[pl.ds(0, devices - 1)],
            send_sem=send_sem.at[phase, chunk],
            recv_sem=recv_sem.at[phase, chunk],
            device_id={"rows": partner_of(me, 1, devices)},
            device_id_type=MESH,
        )

    share = TAIL_X_ROWS // TP

    def fill(chunk, piece, into, at):
        rows = state[given, piece, chunk * PART : (chunk + 1) * PART, :]
        into[at, 0:PART, :] = rows[:, :LANES]
        into[at, PART : 2 * PART, :] = rows[:, LANES:]
        if chunk == 0:
            entry = TAIL_X_ROWS + share * column + lax.rem(piece, share)
            into[at, 2 * PART, :] = tails[jnp.where(piece < TAIL_X_ROWS, piece, entry), :]

    def ready(chunk):
        def one(i, carry):
            to = partner_of(me, i, devices)
            fill(chunk, to, first[chunk], to)
            return carry

        lax.fori_loop(1, devices, one, 0)
        fill(chunk, me, spread[chunk], me)

    loads[3].wait()
    for chunk in range(CHUNKS):
        ready(chunk)
    pl.semaphore_wait(barrier, devices - 1 + TP - 1)
    for chunk in range(CHUNKS):

        def begin(i, carry, chunk=chunk):
            remote(0, chunk, partner_of(me, i, devices)).start()
            return carry

        lax.fori_loop(1, devices, begin, 0)

    for load in loads[4:]:
        load.wait()
    group_of_lane = lax.broadcasted_iota(jnp.int32, (GROUPS, LANES), 1) // PER_GROUP
    own_group = group_of_lane == lax.broadcasted_iota(jnp.int32, (GROUPS, LANES), 0)
    lane = lax.broadcasted_iota(jnp.int32, (8, LANES), 1)

    def by_head(values):
        return jnp.sum(jnp.where(own_group, values, 0.0), axis=0, keepdims=True)

    def prepare(row, slot, window_x, window_bc):
        live = active[slot] == 1
        new_x = [x_new[s, slot].astype(jnp.float32) for s in range(STEPS)]
        new_bc = [
            [bc_new[s, slot, b].astype(jnp.float32) for b in range(2)] for s in range(STEPS)
        ]
        frames_x = window_x + new_x
        frames_bc = window_bc + new_bc
        conv_x = []
        conv_b = []
        conv_c = []
        sizes = []
        decay = []
        rate = jnp.exp(a_log[...])
        for s in range(STEPS):
            total = frames_x[s] * conv_wx[0]
            for k in range(1, 4):
                total = total + frames_x[s + k] * conv_wx[k]
            conv_x.append(silu(total + conv_bx[...]))
            pair = []
            for b in range(2):
                total = frames_bc[s][b] * conv_wbc[0, b]
                for k in range(1, 4):
                    total = total + frames_bc[s + k][b] * conv_wbc[k, b]
                pair.append(silu(total + conv_bbc[b]))
            conv_b.append(pair[0])
            conv_c.append(pair[1])
            raw = jnp.where(slot == 0, dt_new[s, 0:1, :], dt_new[s, 1:2, :]) + dt_bias[...]
            size = jnp.maximum(raw, 0.0) + jnp.log1p(jnp.exp(-jnp.abs(raw)))
            sizes.append(size)
            decay.append(jnp.exp(-size * rate))
            for half in range(2):
                for g in range(GROUPS):
                    at = slice(half * LANES, (half + 1) * LANES)
                    rows_b[row, s, half, g] = jnp.broadcast_to(pair[0][g : g + 1, at], (8, LANES))
                    rows_c[row, s, half, g] = jnp.broadcast_to(pair[1][g : g + 1, at], (8, LANES))
            gates[row, s] = silu(z_new[s, slot].astype(jnp.float32))

        def overlap(i, j):
            return by_head(jnp.sum(conv_b[i] * conv_c[j], axis=1, keepdims=True))

        skip = skip_d[...]
        put_in = [sizes[s] * conv_x[s] for s in range(STEPS)]
        carried = put_in[0] * decay[1]
        both = decay[0] * decay[1]
        decays[row, 0] = jnp.broadcast_to(decay[0], (DEPTH, LANES))
        decays[row, 1] = jnp.broadcast_to(both, (DEPTH, LANES))
        extras[row, 0] = put_in[0] * overlap(0, 0) + skip * conv_x[0]
        extras[row, 1] = (
            carried * overlap(0, 1) + put_in[1] * overlap(1, 1) + skip * conv_x[1]
        )
        turned[0:DEPTH, :] = jnp.where(live, carried, 0.0)
        turned[DEPTH : 2 * DEPTH, :] = jnp.where(live, put_in[1], 0.0)
        turned[2 * DEPTH : 2 * DEPTH + 8, :] = jnp.broadcast_to(
            jnp.where(live, both, 1.0), (8, LANES)
        )
        turned[2 * DEPTH + 8 :, :] = jnp.zeros((LANES - 2 * DEPTH - 8, LANES), jnp.float32)
        factors[row] = jnp.transpose(turned[...])
        for k in range(3):
            at = TAIL_X + (row * 3 + k) * DEPTH
            pack[at : at + DEPTH, :] = jnp.where(live, frames_x[k + 2], frames_x[k])
            for b in range(2):
                entry = jnp.where(live, frames_bc[k + 2][b], frames_bc[k][b])
                at = TAIL_BC + ((row * 3 + k) * 2 + b) * 8
                pack[at : at + 4, :] = entry[:, :LANES]
                pack[at + 4 : at + 8, :] = entry[:, LANES:]

    def readout(row, octets, piece):
        def one_group(g, carry):
            c = [
                [rows_c[row, s, half, g] for half in range(2)] for s in range(STEPS)
            ]
            for octet in octets:
                held = jnp.zeros((8, LANES), jnp.float32)
                for p in range(DEPTH):
                    left, right = piece(GROUPS * p + g, octet)
                    for s in range(STEPS):
                        dot = jnp.sum(
                            left * c[s][0] + right * c[s][1], axis=1, keepdims=True
                        )
                        held = jnp.where(lane == DEPTH * s + p, dot, held)
                at = pl.multiple_of(g * PER_GROUP + octet * 8, 8)
                dots[pl.ds(at, 8), :] = held
            return carry

        lax.fori_loop(0, GROUPS, one_group, 0)

    def update(row, octets, piece):
        def one_group(g, carry):
            b = [[rows_b[row, s, half, g] for half in range(2)] for s in range(STEPS)]
            for octet in octets:
                heads = pl.ds(pl.multiple_of(g * PER_GROUP + octet * 8, 8), 8)

                def spread_out(at):
                    return jnp.broadcast_to(factors[row, heads, at : at + 1], (8, LANES))

                decay = spread_out(2 * DEPTH)
                for p in range(DEPTH):
                    u1 = spread_out(p)
                    u2 = spread_out(DEPTH + p)
                    k = GROUPS * p + g
                    for half, held in enumerate(piece(k, octet)):
                        final[
                            row,
                            k,
                            8 * octet : 8 * octet + 8,
                            half * LANES : (half + 1) * LANES,
                        ] = held * decay + u1 * b[0][half] + u2 * b[1][half]
            return carry

        lax.fori_loop(0, GROUPS, one_group, 0)

    def finish(row):
        by_step = jnp.transpose(dots[...])
        for s in range(STEPS):
            dot = by_step[DEPTH * s : DEPTH * (s + 1), :]
            gated = (decays[row, s] * dot + extras[row, s]) * gates[row, s]
            at = Y_ROWS + (row * STEPS + s) * DEPTH
            pack[at : at + DEPTH, :] = gated
            sums[row * STEPS + s : row * STEPS + s + 1, :] = jnp.sum(
                gated * gated, axis=0, keepdims=True
            )

    prepare(
        0,
        kept_slot,
        [tail_x[kept, k].astype(jnp.float32) for k in range(3)],
        [[tail_bc[kept, k, b].astype(jnp.float32) for b in range(2)] for k in range(3)],
    )
    sums[4:8, :] = jnp.zeros((4, LANES), jnp.float32)

    def kept_piece(at, octet):
        rows = state[kept, at, 8 * octet : 8 * octet + 8, :]
        return rows[:, :LANES], rows[:, LANES:]

    readout(0, range(PER_GROUP // 8), kept_piece)
    finish(0)
    update(0, range(PER_GROUP // 8), kept_piece)
    outs = [
        pltpu.make_async_copy(final.at[0], final_hbm.at[0], out_sem.at[0]),
        pltpu.make_async_copy(pack, pack_hbm, out_sem.at[1]),
    ] + [
        pltpu.make_async_copy(
            final.at[1, :, pl.ds(chunk * PART, PART), :],
            final_hbm.at[1, :, pl.ds(chunk * PART, PART), :],
            out_sem.at[2 + chunk],
        )
        for chunk in range(CHUNKS)
    ] + [pltpu.make_async_copy(sums, sums_hbm.at[0], out_sem.at[2 + CHUNKS])]
    outs[0].start()

    def giver(to):
        from_low = lax.shift_right_logical(source[2 * to], 1)
        from_high = lax.shift_right_logical(source[2 * to + 1], 1)
        return jnp.where(from_low != to, from_low, from_high)

    for chunk in range(CHUNKS):
        all_pieces(0, chunk).wait_recv()

        def forward(i, carry, chunk=chunk):
            to = partner_of(me, i, devices)
            second[chunk][to] = spread[chunk][giver(to)]
            remote(1, chunk, to).start()
            return carry

        lax.fori_loop(1, devices, forward, 0)
        back[chunk][me] = spread[chunk][giver(me)]

    for chunk in range(CHUNKS):
        all_pieces(1, chunk).wait_recv()
        if chunk == 0:

            def untail(k, carry):
                tails[k, :] = back_a[k, 2 * PART, :]
                return carry

            lax.fori_loop(0, devices, untail, 0)
            quarter[...] = tails[TAIL_X_ROWS : TAIL_X_ROWS + 16, :]
            quarters[column] = quarter[...]
            shares = [
                pltpu.make_async_remote_copy(
                    src_ref=quarter,
                    dst_ref=quarters.at[column],
                    send_sem=share_send_sem.at[j - 1],
                    recv_sem=share_recv_sem.at[j - 1],
                    device_id={"tp": lax.rem(column + j, TP)},
                    device_id_type=MESH,
                )
                for j in range(1, TP)
            ]
            for copy in shares:
                copy.start()
            for copy in shares:
                copy.wait()
            for r in range(TAIL_X_ROWS):
                at = TAIL_X_ROWS + r
                tails[at : at + 1, :] = quarters[r // share, r % share : r % share + 1, :]
            window_bc = [
                [
                    jnp.concatenate(
                        [
                            tails[48 + (2 * k + b) * 8 : 52 + (2 * k + b) * 8, :],
                            tails[52 + (2 * k + b) * 8 : 56 + (2 * k + b) * 8, :],
                        ],
                        axis=1,
                    )
                    for b in range(2)
                ]
                for k in range(3)
            ]
            prepare(
                1,
                moved_slot,
                [tails[DEPTH * k : DEPTH * (k + 1), :] for k in range(3)],
                window_bc,
            )

        def moved_piece(at, octet, chunk=chunk):
            within = 8 * octet - PART * chunk
            return (
                back[chunk][at, within : within + 8, :],
                back[chunk][at, PART + within : PART + within + 8, :],
            )

        octets = range(chunk * PART // 8, (chunk + 1) * PART // 8)
        readout(1, octets, moved_piece)
        if chunk < CHUNKS - 1:
            update(1, octets, moved_piece)
            outs[2 + chunk].start()
    finish(1)

    exchanges = [
        pltpu.make_async_remote_copy(
            src_ref=sums,
            dst_ref=sums_hbm.at[j],
            send_sem=sum_send_sem.at[j - 1],
            recv_sem=sum_recv_sem.at[j - 1],
            device_id={"tp": lax.rem(column + j, TP)},
            device_id_type=MESH,
        )
        for j in range(1, TP)
    ]
    for exchange in exchanges:
        exchange.start()
    for at in (1, 2 + CHUNKS):
        outs[at].start()
    update(1, octets, moved_piece)
    outs[1 + CHUNKS].start()
    for exchange in exchanges:
        exchange.wait_recv()
    for exchange in exchanges:
        exchange.wait_send()
    for phase in range(2):
        for chunk in range(CHUNKS):
            all_pieces(phase, chunk).wait_send()
    for out in outs:
        out.wait()


PARTS = 2


def place_kernel(
    devices,
    source_hbm,
    active_hbm,
    norm_gain_hbm,
    sums_hbm,
    final_hbm,
    pack_hbm,
    state_out,
    tail_x_out,
    tail_bc_out,
    y_out,
    source,
    active,
    norm_gain,
    sums,
    held,
    pack,
    tail_x,
    tail_bc,
    y,
    sem,
    part_sem,
):
    me = lax.axis_index("rows")
    size = devices // PARTS
    source_load = pltpu.make_async_copy(source_hbm, source, sem.at[0])
    small_loads = [
        pltpu.make_async_copy(hbm, vmem, sem.at[1 + i])
        for i, (hbm, vmem) in enumerate(
            (
                (sums_hbm, sums),
                (pack_hbm, pack),
                (active_hbm, active),
                (norm_gain_hbm, norm_gain),
            )
        )
    ]
    source_load.start()
    for load in small_loads:
        load.start()
    parts = [(row, q) for row in range(2) for q in range(PARTS)]
    loads = [
        pltpu.make_async_copy(
            final_hbm.at[row, pl.ds(q * size, size)],
            held.at[row, pl.ds(q * size, size)],
            part_sem.at[row, q],
        )
        for row, q in parts
    ]
    for load in loads:
        load.start()
    source_load.wait()
    low = source[2 * me]
    high = source[2 * me + 1]
    kept = 1 - given_of(low, high, me)
    kept_slot = jnp.where(low == 2 * me + kept, 0, 1)
    slots = (kept_slot, 1 - kept_slot)
    writes = []
    for load, (row, q) in zip(loads, parts):
        load.wait()
        write = pltpu.make_async_copy(
            held.at[row, pl.ds(q * size, size)],
            state_out.at[slots[row], pl.ds(q * size, size)],
            part_sem.at[2 + row, q],
        )
        write.start()
        writes.append(write)
    for load in small_loads:
        load.wait()
    same_group = (
        lax.broadcasted_iota(jnp.int32, (LANES, LANES), 0) // PER_GROUP
        == lax.broadcasted_iota(jnp.int32, (LANES, LANES), 1) // PER_GROUP
    ).astype(jnp.float32)
    totals = jnp.dot(
        sums[0] + sums[1] + sums[2] + sums[3],
        same_group,
        preferred_element_type=jnp.float32,
        precision=lax.Precision.HIGHEST,
    )
    factor = lax.rsqrt(totals / (DEPTH * TP * PER_GROUP) + EPSILON)
    for row, slot in enumerate(slots):
        live = active[slot] == 1
        for s in range(STEPS):
            scale = factor[row * STEPS + s : row * STEPS + s + 1, :]
            at = Y_ROWS + (row * STEPS + s) * DEPTH
            scaled = pack[at : at + DEPTH, :] * scale * norm_gain[...]
            y[s, slot] = jnp.where(live, scaled, 0.0).astype(jnp.bfloat16)
        for k in range(3):
            at = TAIL_X + (row * 3 + k) * DEPTH
            tail_x[slot, k] = pack[at : at + DEPTH, :].astype(jnp.bfloat16)
            for c in range(2):
                at = TAIL_BC + ((row * 3 + k) * 2 + c) * 8
                tail_bc[slot, k, c] = jnp.concatenate(
                    [pack[at : at + 4, :], pack[at + 4 : at + 8, :]], axis=1
                ).astype(jnp.bfloat16)
    for i, (vmem, hbm) in enumerate(((tail_x, tail_x_out), (tail_bc, tail_bc_out), (y, y_out))):
        write = pltpu.make_async_copy(vmem, hbm, sem.at[5 + i])
        write.start()
        writes.append(write)
    for write in writes:
        write.wait()


def on_device(
    state_in,
    tail_x,
    tail_bc,
    source,
    active,
    x_new,
    z_new,
    bc_new,
    dt_new,
    conv_wx,
    conv_bx,
    conv_wbc,
    conv_bbc,
    dt_bias,
    a_log,
    skip_d,
    norm_gain,
):
    devices = lax.axis_size("rows")
    slots, depth, head_count, width = state_in.shape
    pieces = state_in.reshape(slots, devices, PER_GROUP, width)
    operands = (
        source,
        active,
        pieces,
        tail_x,
        tail_bc,
        x_new,
        z_new,
        bc_new,
        dt_new,
        conv_wx,
        conv_bx,
        conv_wbc,
        conv_bbc,
        dt_bias.reshape(1, -1),
        a_log.reshape(1, -1),
        skip_d.reshape(1, -1),
    )
    long_buffer = pltpu.VMEM((devices, 2 * PART + 1, LANES), jnp.float32)
    short_buffer = pltpu.VMEM((devices, 2 * PART, LANES), jnp.float32)
    hbm = pl.BlockSpec(memory_space=pltpu.HBM)
    final, pack, sums = pl.pallas_call(
        functools.partial(relocate_kernel, devices),
        out_shape=(
            jax.ShapeDtypeStruct(pieces.shape, jnp.float32),
            jax.ShapeDtypeStruct((PACK_ROWS, LANES), jnp.float32),
            jax.ShapeDtypeStruct((TP, 8, LANES), jnp.float32),
        ),
        in_specs=[hbm] * len(operands),
        out_specs=(hbm, hbm, hbm),
        scratch_shapes=[
            pltpu.SMEM(source.shape, jnp.int32),
            pltpu.SMEM(active.shape, jnp.int32),
        ]
        + [pltpu.VMEM(a.shape, a.dtype) for a in operands[2:]]
        + [
            pltpu.VMEM((2 * TAIL_X_ROWS, LANES), jnp.float32),
            pltpu.VMEM((16, LANES), jnp.float32),
            pltpu.VMEM((TP, 16, LANES), jnp.float32),
        ]
        + [long_buffer, short_buffer] * 4
        + [
            pltpu.VMEM((PACK_ROWS, LANES), jnp.float32),
            pltpu.VMEM(pieces.shape, jnp.float32),
            pltpu.VMEM((2, STEPS, 2, GROUPS, 8, LANES), jnp.float32),
            pltpu.VMEM((2, STEPS, 2, GROUPS, 8, LANES), jnp.float32),
            pltpu.VMEM((2, LANES, LANES), jnp.float32),
            pltpu.VMEM((2, STEPS, DEPTH, LANES), jnp.float32),
            pltpu.VMEM((2, STEPS, DEPTH, LANES), jnp.float32),
            pltpu.VMEM((2, STEPS, DEPTH, LANES), jnp.float32),
            pltpu.VMEM((LANES, LANES), jnp.float32),
            pltpu.VMEM((LANES, LANES), jnp.float32),
            pltpu.VMEM((8, LANES), jnp.float32),
            pltpu.SemaphoreType.DMA((len(operands),)),
            pltpu.SemaphoreType.DMA((2, CHUNKS)),
            pltpu.SemaphoreType.DMA((2, CHUNKS)),
            pltpu.SemaphoreType.DMA((TP - 1,)),
            pltpu.SemaphoreType.DMA((TP - 1,)),
            pltpu.SemaphoreType.DMA((TP - 1,)),
            pltpu.SemaphoreType.DMA((TP - 1,)),
            pltpu.SemaphoreType.DMA((3 + CHUNKS,)),
        ],
        compiler_params=pltpu.CompilerParams(
            collective_id=0, has_side_effects=True, vmem_limit_bytes=60 * 1024 * 1024
        ),
    )(*operands)
    state, window_x, window_bc, y = pl.pallas_call(
        functools.partial(place_kernel, devices),
        out_shape=(
            jax.ShapeDtypeStruct(pieces.shape, jnp.float32),
            jax.ShapeDtypeStruct(tail_x.shape, tail_x.dtype),
            jax.ShapeDtypeStruct(tail_bc.shape, tail_bc.dtype),
            jax.ShapeDtypeStruct(x_new.shape, jnp.bfloat16),
        ),
        in_specs=[hbm] * 6,
        out_specs=(hbm,) * 4,
        scratch_shapes=[
            pltpu.SMEM(source.shape, jnp.int32),
            pltpu.SMEM(active.shape, jnp.int32),
            pltpu.VMEM(norm_gain.shape, jnp.float32),
            pltpu.VMEM((TP, 8, LANES), jnp.float32),
            pltpu.VMEM(pieces.shape, jnp.float32),
            pltpu.VMEM((PACK_ROWS, LANES), jnp.float32),
            pltpu.VMEM(tail_x.shape, tail_x.dtype),
            pltpu.VMEM(tail_bc.shape, tail_bc.dtype),
            pltpu.VMEM(x_new.shape, jnp.bfloat16),
            pltpu.SemaphoreType.DMA((8,)),
            pltpu.SemaphoreType.DMA((4, PARTS)),
        ],
        compiler_params=pltpu.CompilerParams(vmem_limit_bytes=60 * 1024 * 1024),
    )(source, active, norm_gain, sums, final, pack)
    return state.reshape(state_in.shape), window_x, window_bc, y


def solution(mesh):
    return jax.shard_map(
        on_device,
        mesh=mesh,
        in_specs=(
            P("rows", "tp", None, None),
            P("rows", None, "tp", None),
            P("rows", None, None, None, None),
            P(),
            P("rows"),
            P(None, "rows", "tp", None),
            P(None, "rows", "tp", None),
            P(None, "rows", None, None, None),
            P(None, "rows", None),
            P(None, "tp", None),
            P("tp", None),
            P(),
            P(),
            P(),
            P(),
            P(),
            P("tp", None),
        ),
        out_specs=(
            P("rows", "tp", None, None),
            P("rows", None, "tp", None),
            P("rows", None, None, None, None),
            P(None, "rows", "tp", None),
        ),
        check_vma=False,
    )
```
